32 devices in a mesh: dp: 8 (over z, x), mp: 4 (over y, core).
Axes of the slice: x: 2, y: 2, z: 4, core: 2. Of those that a mesh axis runs over, the one named last changes fastest.
Arguments:
- tokens: bfloat16 [8192, 2048], P('dp'), may hold values from -6 to 6
- cotangent: bfloat16 [8192, 2048], P('dp'), may hold values from -6 to 6
- seq_level: int32 [8], P('dp'), may hold values from 0 to 3, as said below
- w_zx: float32 [2048, 2, 4096], P('dp', None, 'mp'), may hold values from -0.125 to 0.125
- w_dt: float32 [2048, 64], P('dp', 'mp'), may hold values from -0.125 to 0.125
- w_bc: float32 [2048, 256], P('dp'), may hold values from -0.125 to 0.125
- w_out: float32 [2048, 4096], P('dp', 'mp'), may hold values from -0.1875 to 0.1875
- vectors: float32 [28096], replicated, may hold values from -7 to 3, as said below
- m_zx: float32 [2048, 2, 4096], P('dp', None, 'mp'), may hold values from -0.00012207031 to 0.00012207031
- m_dt: float32 [2048, 64], P('dp', 'mp'), may hold values from -0.00012207031 to 0.00012207031
- m_bc: float32 [2048, 256], P('dp'), may hold values from -0.00012207031 to 0.00012207031
- m_out: float32 [2048, 4096], P('dp', 'mp'), may hold values from -0.00012207031 to 0.00012207031
- m_vec: float32 [28096], replicated, may hold values from -0.00048828125 to 0.00048828125
- v_zx: float32 [2048, 2, 4096], P('dp', None, 'mp'), may hold values from 2.034873e-09 to 8.124017e-09
- v_dt: float32 [2048, 64], P('dp', 'mp'), may hold values from 2.034873e-09 to 8.124017e-09
- v_bc: float32 [2048, 256], P('dp'), may hold values from 2.034873e-09 to 8.124017e-09
- v_out: float32 [2048, 4096], P('dp', 'mp'), may hold values from 2.034873e-09 to 8.124017e-09
- v_vec: float32 [28096], replicated, may hold values from 3.2496068e-08 to 1.3037113e-07
Outputs:
- block_out: bfloat16 [8192, 2048], P('dp')
- input_grad: bfloat16 [8192, 2048], P('dp')
- grad_norm: float32 [], replicated
- new_w_zx: float32 [2048, 2, 4096], P('dp', None, 'mp')
- new_m_zx: float32 [2048, 2, 4096], P('dp', None, 'mp')
- new_v_zx: float32 [2048, 2, 4096], P('dp', None, 'mp')
- new_w_dt: float32 [2048, 64], P('dp', 'mp')
- new_m_dt: float32 [2048, 64], P('dp', 'mp')
- new_v_dt: float32 [2048, 64], P('dp', 'mp')
- new_w_bc: float32 [2048, 256], P('dp')
- new_m_bc: float32 [2048, 256], P('dp')
- new_v_bc: float32 [2048, 256], P('dp')
- new_w_out: float32 [2048, 4096], P('dp', 'mp')
- new_m_out: float32 [2048, 4096], P('dp', 'mp')
- new_v_out: float32 [2048, 4096], P('dp', 'mp')
- new_vectors: float32 [28096], replicated
- new_m_vec: float32 [28096], replicated
- new_v_vec: float32 [28096], replicated
The draws below stay inside these ranges and needn't reach their ends.
Inputs may be any that keep to these rules, and one draw needn't show every extreme that they name: `seq_level`: level k makes the first 2**k * 8 heads live; some sequence has level 3 and some has level 0. `vectors`: laid out as the steps say.
All inputs are finite; a program needn't handle non-finite values.
Results may differ from the reference program's by a relative error of at most 0.0097.
Values may be sent and summed in bfloat16 or wider, within the bound.
A program may use at most 320 MiB of HBM per device.

```python
import math
import jax
import jax.numpy as jnp
from jax import lax

D = 2048
H = 64
HD = 64
N = 128
CONV = 4
GROUP = 256
LEN = 1024
STEP = 10
DI = 4096
SEQS = 8
TOKENS = 8192
NV = 28096
NPARAM = 25849280


def draw_seq_level(key, part):
    key = jax.random.fold_in(key, 3)
    sub_keys = jax.random.split(key, 3)
    buckets = jax.random.randint(sub_keys[0], (SEQS,), 0, 38)
    levels = (buckets >= 16).astype(jnp.int32) + (buckets >= 26).astype(jnp.int32) + (buckets >= 34).astype(jnp.int32)
    first_pick = jax.random.randint(sub_keys[1], (), 0, SEQS)
    second_pick = (first_pick + 1 + jax.random.randint(sub_keys[2], (), 0, SEQS - 1)) % SEQS
    levels = levels.at[first_pick].set(3)
    levels = levels.at[second_pick].set(0)
    return levels.astype(jnp.int32)


def draw_vectors(key, part):
    key = jax.random.fold_in(key, 11)
    sub_keys = jax.random.split(key, 9)
    inner = H * HD
    ramp_in = 0.6 + 1.2 * jnp.arange(D, dtype=jnp.float32) / D
    gain_in = ramp_in * jax.random.uniform(sub_keys[0], (D,), jnp.float32, 0.7, 1.3)
    chan_taps = jax.random.uniform(sub_keys[1], (CONV * inner,), jnp.float32, -0.5, 0.5)
    chan_bias = jax.random.uniform(sub_keys[2], (inner,), jnp.float32, -0.5, 0.5)
    ramp_gate = 0.5 + 1.5 * jnp.arange(inner, dtype=jnp.float32) / inner
    gate_gain = ramp_gate * jax.random.uniform(sub_keys[3], (inner,), jnp.float32, 0.7, 1.3)
    state_taps = jax.random.uniform(sub_keys[4], (CONV * 2 * N,), jnp.float32, -0.5, 0.5)
    state_bias = jax.random.uniform(sub_keys[5], (2 * N,), jnp.float32, -0.5, 0.5)
    dt_bias = jax.random.uniform(sub_keys[6], (H,), jnp.float32, -6.0, -2.0)
    a_log = jax.random.uniform(sub_keys[7], (H,), jnp.float32, 0.0, 2.77)
    skip_gain = jax.random.uniform(sub_keys[8], (H,), jnp.float32, 0.5, 1.5)
    return jnp.concatenate([gain_in, chan_taps, chan_bias, gate_gain, state_taps, state_bias, dt_bias, a_log, skip_gain])


def block_scale(rng, extent, shards, low, top_value):
    factor_of = 1.0
    for dim, shards_of in shards:
        draws = jax.random.uniform(jax.random.fold_in(jax.random.fold_in(rng, 6), dim), (shards_of,), jnp.float32, low / len(shards), top_value / len(shards))
        factor_of = factor_of * jnp.repeat(jnp.exp(draws), extent[dim] // shards_of).reshape((-1,) + (1,) * (len(extent) - 1 - dim))
    return factor_of


def bell_draw(stream_key, shape, spread, bound, cuts=(), kind=jnp.bfloat16):
    values = jax.random.normal(stream_key, shape, jnp.float32) * spread
    if len(cuts) > 0:
        values = block_scale(stream_key, shape, cuts, -0.22, 0.18) * values
    return jnp.clip(values, min=-bound, max=bound).astype(kind)


def setup_inputs(seed: int = 0) -> dict:
    splits = jax.random.split(jax.random.key(seed), 19)
    return {
        "tokens": bell_draw(splits[0], (TOKENS, D), 1.0, 6.0, ((0, 8),)),
        "cotangent": bell_draw(splits[1], (TOKENS, D), 1.0, 6.0, ((0, 8),)),
        "seq_level": draw_seq_level(jax.random.fold_in(splits[18], 71), 0),
        "w_zx": bell_draw(splits[3], (D, 2, DI), D ** -0.5, 0.125, ((0, 8), (2, 4)), jnp.float32),
        "w_dt": bell_draw(splits[4], (D, H), D ** -0.5, 0.125, ((0, 8), (1, 4)), jnp.float32),
        "w_bc": bell_draw(splits[5], (D, 2 * N), D ** -0.5, 0.125, ((0, 8),), jnp.float32),
        "w_out": bell_draw(splits[6], (D, DI), (DI // 4) ** -0.5, 0.1875, ((0, 8), (1, 4)), jnp.float32),
        "vectors": draw_vectors(jax.random.fold_in(splits[18], 71), 0),
        "m_zx": bell_draw(splits[8], (D, 2, DI), (0.111 * NPARAM ** -0.5), 0.00012207031, ((0, 8), (2, 4)), jnp.float32),
        "m_dt": bell_draw(splits[9], (D, H), (0.111 * NPARAM ** -0.5), 0.00012207031, ((0, 8), (1, 4)), jnp.float32),
        "m_bc": bell_draw(splits[10], (D, 2 * N), (0.111 * NPARAM ** -0.5), 0.00012207031, ((0, 8),), jnp.float32),
        "m_out": bell_draw(splits[11], (D, DI), (0.111 * NPARAM ** -0.5), 0.00012207031, ((0, 8), (1, 4)), jnp.float32),
        "m_vec": bell_draw(splits[12], (NV,), (0.44 * NPARAM ** -0.5), 0.00048828125, (), jnp.float32),
        "v_zx": jnp.clip(jnp.exp(math.log(8.124017014665696e-09) - 1.38439136 * jax.random.uniform(splits[13], (D, 2, DI), jnp.float32) ** block_scale(splits[13], (D, 2, DI), ((0, 8), (2, 4)), -0.2, 0.2)), 2.034872936818033e-09, 8.124017014665696e-09),
        "v_dt": jnp.clip(jnp.exp(math.log(8.124017014665696e-09) - 1.38439136 * jax.random.uniform(splits[14], (D, H), jnp.float32) ** block_scale(splits[14], (D, H), ((0, 8), (1, 4)), -0.2, 0.2)), 2.034872936818033e-09, 8.124017014665696e-09),
        "v_bc": jnp.clip(jnp.exp(math.log(8.124017014665696e-09) - 1.38439136 * jax.random.uniform(splits[15], (D, 2 * N), jnp.float32) ** block_scale(splits[15], (D, 2 * N), ((0, 8),), -0.2, 0.2)), 2.034872936818033e-09, 8.124017014665696e-09),
        "v_out": jnp.clip(jnp.exp(math.log(8.124017014665696e-09) - 1.38439136 * jax.random.uniform(splits[16], (D, DI), jnp.float32) ** block_scale(splits[16], (D, DI), ((0, 8), (1, 4)), -0.2, 0.2)), 2.034872936818033e-09, 8.124017014665696e-09),
        "v_vec": jnp.clip(jnp.exp(jax.random.uniform(splits[17], (NV,), jnp.float32, math.log(3.2496068058662786e-08), math.log(1.303711343325631e-07))), 3.2496068058662786e-08, 1.303711343325631e-07),
    }


EPS = 1e-05
CLIP = 1.0
BETA_FIRST = 0.9
BETA_SECOND = 0.95
ADAM_EPS = 1e-08
RATE_MATRIX = 0.03
RATE_VECTOR = 0.3
DECAY_MATRIX = 0.1
HIGH = lax.Precision.HIGHEST

@jax.custom_vjp
def low(v):
    return lax.optimization_barrier(v.astype(jnp.bfloat16)).astype(jnp.float32)

@jax.custom_vjp
def low_back(v):
    return v

def low_keep(v):
    return (low(v), None)

def low_pass(kept, grad):
    return (grad,)

def back_keep(v):
    return (v, None)

def back_low(kept, grad):
    return (low(grad),)
low.defvjp(low_keep, low_pass)
low_back.defvjp(back_keep, back_low)

def input_norm(inputs, gain_in):
    mean_square = lax.optimization_barrier(jnp.mean(inputs * inputs, axis=-1, keepdims=True))
    return inputs * lax.rsqrt(mean_square + EPS) * gain_in

def causal_conv(values, tap_rows, offset):
    length = values.shape[0]
    padded = jnp.concatenate([jnp.zeros((CONV - 1, values.shape[1]), jnp.float32), values], axis=0)
    summed = offset + tap_rows[0] * padded[0:length]
    for tap_index in range(1, CONV):
        summed = summed + tap_rows[tap_index] * padded[tap_index:tap_index + length]
    return jax.nn.silu(summed)

def group_scan(inputs, steps_dt, log_decay, b_rows, c_rows):
    length, head_count, head_dim = inputs.shape
    state_dim = b_rows.shape[1]
    blocks = length // GROUP
    x_blk = inputs.reshape(blocks, GROUP, head_count, head_dim)
    dt_blk = steps_dt.reshape(blocks, GROUP, head_count)
    cum_log = jnp.cumsum(log_decay.reshape(blocks, GROUP, head_count), axis=1)
    b_blk = b_rows.reshape(blocks, GROUP, state_dim)
    c_blk = c_rows.reshape(blocks, GROUP, state_dim)
    scores = jnp.einsum('cin,cjn->cij', c_blk, b_blk, precision=HIGH)
    causal = (jnp.arange(GROUP)[:, None] >= jnp.arange(GROUP)[None, :])[None, :, :, None]
    log_gaps = cum_log[:, :, None, :] - cum_log[:, None, :, :]
    mixing = jnp.where(causal, jnp.exp(jnp.where(causal, log_gaps, 0.0)), 0.0)
    mixing = mixing * scores[:, :, :, None] * dt_blk[:, None, :, :]
    y_diag = jnp.einsum('cijh,cjhp->cihp', mixing, x_blk, precision=HIGH)
    tail_weight = jnp.exp(cum_log[:, -1:, :] - cum_log) * dt_blk
    weighted_x = tail_weight[:, :, :, None] * x_blk
    block_state = jnp.einsum('cjhp,cjn->chpn', weighted_x, b_blk, precision=HIGH)

    def advance(state_in, pieces):
        new_state, total_log = pieces
        return (state_in * jnp.exp(total_log)[:, None, None] + new_state, state_in)
    start_state = jnp.zeros((head_count, head_dim, state_dim), jnp.float32)
    _, incoming = lax.scan(advance, start_state, (block_state, cum_log[:, -1, :]))
    y_off = jnp.einsum('cin,chpn->cihp', c_blk, incoming, precision=HIGH) * jnp.exp(cum_log)[:, :, :, None]
    return (y_diag + y_off).reshape(length, head_count, head_dim)

def mixer(z_part, x_part, dt_part, bc_part, chan_part, state_part, head_part, mask_row):
    length = x_part.shape[0]
    state_dim = bc_part.shape[1] // 2
    head_count = head_part.shape[1]
    conv_x = causal_conv(x_part, chan_part[:CONV], chan_part[CONV])
    conv_bc = causal_conv(bc_part, state_part[:CONV], state_part[CONV])
    steps_dt = jax.nn.softplus(dt_part + head_part[0])
    log_decay = -jnp.exp(head_part[1]) * steps_dt
    x_heads = conv_x.reshape(length, head_count, -1)
    scanned = group_scan(x_heads, steps_dt, log_decay, conv_bc[:, :state_dim], conv_bc[:, state_dim:])
    mixed = (scanned + head_part[2][:, None] * x_heads) * mask_row[:, None]
    return mixed.reshape(length, -1) * jax.nn.silu(z_part)

def sequence_forward(seq_tokens, level, w_zx, w_dt, w_bc, w_out, vectors):
    inner = H * HD
    gain_in = vectors[:D]
    chan_all = vectors[D:D + 6 * inner].reshape(6, inner)
    state_start = D + 6 * inner
    state_vec = vectors[state_start:state_start + 10 * N].reshape(5, 2 * N)
    head_start = state_start + 10 * N
    head_vec = vectors[head_start:head_start + 3 * H].reshape(3, H)
    normed = input_norm(seq_tokens, gain_in)
    quant = low(normed)
    proj = low_back(jnp.einsum('td,dkc->tkc', quant, low(w_zx), precision=HIGH))
    dt_raw = low_back(jnp.dot(quant, low(w_dt), precision=HIGH))
    bc_raw = low_back(jnp.dot(quant, low(w_bc), precision=HIGH))
    active = jnp.left_shift(jnp.int32(H // 8), level)
    head_mask = (jnp.arange(H) < active).astype(jnp.float32)
    gated = mixer(proj[:, 0], proj[:, 1], dt_raw, bc_raw, chan_all[:5], state_vec, head_vec, head_mask)
    sum_sq = lax.optimization_barrier(jnp.sum(gated * gated, axis=-1, keepdims=True))
    scale = lax.rsqrt(sum_sq / (active * HD).astype(jnp.float32) + EPS)
    normed_out = low(gated * scale * chan_all[5])
    return seq_tokens + jnp.dot(normed_out, low(w_out).T, precision=HIGH)

def adam_step(weight, grad, first, second, rate, shrink):
    first = BETA_FIRST * first + (1.0 - BETA_FIRST) * grad
    second = BETA_SECOND * second + (1.0 - BETA_SECOND) * grad * grad
    fix_first = 1.0 - BETA_FIRST ** STEP
    fix_second = 1.0 - BETA_SECOND ** STEP
    update = first / fix_first / (jnp.sqrt(second / fix_second) + ADAM_EPS) + shrink * weight
    return (weight - rate * update, first, second)

def reference(tokens, cotangent, seq_level, w_zx, w_dt, w_bc, w_out, vectors, m_zx, m_dt, m_bc, m_out, m_vec, v_zx, v_dt, v_bc, v_out, v_vec):

    def forward(tok_all, wzx_all, wdt_all, wbc_all, wout_all, vec_all):
        seq_tokens = tok_all.reshape(SEQS, LEN, D)

        def one_seq(pieces):
            return sequence_forward(pieces[0], pieces[1], wzx_all, wdt_all, wbc_all, wout_all, vec_all)
        outputs = lax.map(jax.checkpoint(one_seq), (seq_tokens, seq_level))
        return outputs.reshape(SEQS * LEN, D)
    tok_f32 = tokens.astype(jnp.float32)
    block, pull_back = jax.vjp(forward, tok_f32, w_zx, w_dt, w_bc, w_out, vectors)
    d_tok, g_zx, g_dt, g_bc, g_out, g_vec = pull_back(cotangent.astype(jnp.float32))
    squares = jnp.sum(g_zx * g_zx) + jnp.sum(g_dt * g_dt) + jnp.sum(g_bc * g_bc) + jnp.sum(g_out * g_out) + jnp.sum(g_vec * g_vec)
    grad_norm = jnp.sqrt(squares)
    clip = CLIP / jnp.maximum(grad_norm, CLIP)
    new_zx = adam_step(w_zx, g_zx * clip, m_zx, v_zx, RATE_MATRIX, DECAY_MATRIX)
    new_dt = adam_step(w_dt, g_dt * clip, m_dt, v_dt, RATE_MATRIX, DECAY_MATRIX)
    new_bc = adam_step(w_bc, g_bc * clip, m_bc, v_bc, RATE_MATRIX, DECAY_MATRIX)
    new_out = adam_step(w_out, g_out * clip, m_out, v_out, RATE_MATRIX, DECAY_MATRIX)
    new_vec = adam_step(vectors, g_vec * clip, m_vec, v_vec, RATE_VECTOR, 0.0)
    return (block.astype(jnp.bfloat16), d_tok.astype(jnp.bfloat16), grad_norm, new_zx[0], new_zx[1], new_zx[2], new_dt[0], new_dt[1], new_dt[2], new_bc[0], new_bc[1], new_bc[2], new_out[0], new_out[1], new_out[2], new_vec[0], new_vec[1], new_vec[2])
```

```python
import functools

import jax
import jax.numpy as jnp
from jax import lax
from jax.experimental import pallas as pl
from jax.experimental.pallas import tpu as pltpu
from jax.sharding import PartitionSpec as P

CONV = 4
STEP = 10


EPS = 1e-05
CLIP = 1.0
BETA_FIRST = 0.9
BETA_SECOND = 0.95
ADAM_EPS = 1e-08
RATE_MATRIX = 0.03
RATE_VECTOR = 0.3
DECAY_MATRIX = 0.1


Q = 128
PAIR = 128
LOG2E = 1.4426950408889634
BF = jnp.bfloat16
F32 = jnp.float32


def dotf(a, b, dims=((1,), (0,))):
    return lax.dot_general(a, b, (dims, ((), ())), preferred_element_type=F32)


def dot_exact(a, b):
    return lax.dot_general(
        a, b, (((1,), (0,)), ((), ())), preferred_element_type=F32, precision=lax.Precision.HIGHEST
    )


def softplus(v):
    return jnp.maximum(v, 0.0) + jnp.log(1.0 + jnp.exp(-jnp.abs(v)))


def sigmoid(v):
    return 1.0 / (1.0 + jnp.exp(-v))


def conv_rows(buf, taps, lanes):
    total = taps[CONV : CONV + 1, lanes]
    for k in range(CONV):
        total = total + taps[k : k + 1, lanes] * buf[5 + k : 5 + k + Q, lanes]
    return total


def steps_of(dt_raw, head):
    dt = softplus(dt_raw + head[0:1, :])
    a2 = -jnp.exp(head[1:2, :]) * dt * LOG2E
    rows = lax.broadcasted_iota(jnp.int32, (Q, Q), 0)
    cols = lax.broadcasted_iota(jnp.int32, (Q, Q), 1)
    tri = (rows >= cols).astype(F32)
    return dt, a2, dot_exact(tri, a2), tri


def pick(col0, col1, first):
    return jnp.where(first, col0, col1)


def scan_fwd_block(c, inner, xdb, chan, state_p, head, hrow, y, states, xbuf, bcbuf, s_ref):
    here = pl.ds(pl.multiple_of(c * Q, Q), Q)
    bc_at = inner + 128

    @pl.when(c == 0)
    def _():
        xbuf[0:8, :] = jnp.zeros((8, inner), F32)
        bcbuf[0:8, :] = jnp.zeros((8, 256), F32)
        s_ref[...] = jnp.zeros_like(s_ref)

    @pl.when(c > 0)
    def _():
        xbuf[0:8, :] = xbuf[Q : Q + 8, :]
        bcbuf[0:8, :] = bcbuf[Q : Q + 8, :]

    xbuf[8:, :] = xdb[:, 0:inner]
    bcbuf[8:, :] = xdb[:, bc_at : bc_at + 256]
    u_bc = conv_rows(bcbuf, state_p, slice(0, 256))
    bc = u_bc * sigmoid(u_bc)
    b_low, c_low = bc[:, :128].astype(BF), bc[:, 128:].astype(BF)
    bt_low = bc[:, :128].T.astype(BF)
    dt, _, cum, tri = steps_of(xdb[:, inner : inner + 128], head)
    cum_t = cum.T
    total = cum[Q - 1 : Q, :]
    grow = jnp.exp2(cum)
    tail = jnp.exp2(total - cum)
    scores = dotf(c_low, b_low, ((1,), (1,))) * tri
    states[0] = s_ref[...].astype(BF)
    first = lax.broadcasted_iota(jnp.int32, (Q, PAIR), 1) < 64
    for p in range(inner // PAIR):
        lanes = slice(p * PAIR, (p + 1) * PAIR)
        h0, h1 = slice(2 * p, 2 * p + 1), slice(2 * p + 1, 2 * p + 2)
        u = conv_rows(xbuf, chan, lanes)
        xc = u * sigmoid(u)
        xd = xc * pick(dt[:, h0], dt[:, h1], first)
        xd_low = xd.astype(BF)
        zero = jnp.zeros_like(xd_low)
        m0 = (jnp.exp2(jnp.minimum(cum[:, h0] - cum_t[h0, :], 0.0)) * scores).astype(BF)
        m1 = (jnp.exp2(jnp.minimum(cum[:, h1] - cum_t[h1, :], 0.0)) * scores).astype(BF)
        out = dotf(m0, jnp.where(first, xd_low, zero)) + dotf(m1, jnp.where(first, zero, xd_low))
        s_in = s_ref[:, lanes]
        out = out + dotf(c_low, s_in.astype(BF)) * pick(grow[:, h0], grow[:, h1], first)
        xt = (xd * pick(tail[:, h0], tail[:, h1], first)).astype(BF)
        last = pick(grow[Q - 1 : Q, h0], grow[Q - 1 : Q, h1], first[0:1, :])
        s_ref[:, lanes] = s_in * last + dotf(bt_low, xt)
        y[here, lanes] = (out + hrow[0:1, lanes] * xc) * hrow[1:2, lanes]


def fold8(v):
    return jnp.sum(v.reshape(Q // 8, 8, v.shape[1]), axis=0)


def back_conv(dbuf, taps, lanes):
    total = taps[CONV - 1 : CONV, lanes] * dbuf[0:Q, lanes]
    for k in range(CONV - 1):
        total = total + taps[k : k + 1, lanes] * dbuf[3 - k : 3 - k + Q, lanes]
    return total


def scan_bwd_kernel(
    inner, blocks, xdb, before, dy, states, chan, state_p, head, hrow,
    dxdb, g_chan, g_state, g_head, g_row,
    xbuf, bcbuf, dubuf, dubc, ds_ref, q_ref, r_ref,
):
    step = pl.program_id(0)
    c = blocks - 1 - step
    bc_at = inner + 128

    @pl.when(step == 0)
    def _():
        dubuf[Q:, :] = jnp.zeros((8, inner), F32)
        dubc[Q:, :] = jnp.zeros((8, 256), F32)
        ds_ref[...] = jnp.zeros_like(ds_ref)
        g_chan[...] = jnp.zeros_like(g_chan)
        g_state[...] = jnp.zeros_like(g_state)
        g_head[...] = jnp.zeros_like(g_head)
        g_row[...] = jnp.zeros_like(g_row)

    @pl.when(step > 0)
    def _():
        dubuf[Q:, :] = dubuf[0:8, :]
        dubc[Q:, :] = dubc[0:8, :]

    keep = (c > 0).astype(F32)
    xbuf[0:8, :] = before[:, 0:inner] * keep
    bcbuf[0:8, :] = before[:, bc_at : bc_at + 256] * keep
    xbuf[8:, :] = xdb[:, 0:inner]
    bcbuf[8:, :] = xdb[:, bc_at : bc_at + 256]
    u_bc = conv_rows(bcbuf, state_p, slice(0, 256))
    sig_bc = sigmoid(u_bc)
    bc = u_bc * sig_bc
    b_low, c_low = bc[:, :128].astype(BF), bc[:, 128:].astype(BF)
    ct_low = bc[:, 128:].T.astype(BF)
    dt_in = xdb[:, inner : inner + 128]
    dt, a2, cum, tri = steps_of(dt_in, head)
    cum_t = cum.T
    total = cum[Q - 1 : Q, :]
    grow = jnp.exp2(cum)
    tail = jnp.exp2(total - cum)
    scores = dotf(c_low, b_low, ((1,), (1,))) * tri
    first = lax.broadcasted_iota(jnp.int32, (Q, PAIR), 1) < 64
    d_scores = jnp.zeros((Q, Q), F32)
    d_c = jnp.zeros((Q, 128), F32)
    d_b = jnp.zeros((Q, 128), F32)
    for p in range(inner // PAIR):
        lanes = slice(p * PAIR, (p + 1) * PAIR)
        h0, h1 = slice(2 * p, 2 * p + 1), slice(2 * p + 1, 2 * p + 2)
        u = conv_rows(xbuf, chan, lanes)
        sig = sigmoid(u)
        xc = u * sig
        dte = pick(dt[:, h0], dt[:, h1], first)
        xd = xc * dte
        xd_low = xd.astype(BF)
        zero = jnp.zeros_like(xd_low)
        x0, x1 = jnp.where(first, xd_low, zero), jnp.where(first, zero, xd_low)
        g_low = dy[:, lanes]
        g = g_low.astype(F32)
        g0, g1 = jnp.where(first, g_low, zero), jnp.where(first, zero, g_low)
        l0 = jnp.exp2(jnp.minimum(cum[:, h0] - cum_t[h0, :], 0.0))
        l1 = jnp.exp2(jnp.minimum(cum[:, h1] - cum_t[h1, :], 0.0))
        m0, m1 = (l0 * scores).astype(BF), (l1 * scores).astype(BF)
        d_scores = d_scores + l0 * dotf(g0, xd_low, ((1,), (1,))) + l1 * dotf(g1, xd_low, ((1,), (1,)))
        y_diag = dotf(m0, x0) + dotf(m1, x1)
        u_diag = dotf(m0, g0, ((0,), (0,))) + dotf(m1, g1, ((0,), (0,)))
        grow_e = pick(grow[:, h0], grow[:, h1], first)
        tail_e = pick(tail[:, h0], tail[:, h1], first)
        last = grow_e[Q - 1 : Q, :]
        s_low = states[0, :, lanes]
        ds = ds_ref[:, lanes]
        ds_low = ds.astype(BF)
        eg_low = (g * grow_e).astype(BF)
        y_off = dotf(c_low, s_low) * grow_e
        d_c = d_c + dotf(eg_low, s_low, ((1,), (1,)))
        u_state = dotf(b_low, ds_low) * tail_e
        xt_low = (xd * tail_e).astype(BF)
        d_b = d_b + dotf(xt_low, ds_low, ((1,), (1,)))
        u_all = u_diag + u_state
        xdf = xd_low.astype(F32)
        d_xc = dte * u_all + hrow[0:1, lanes] * g
        q_ref[:, lanes] = g * (y_diag + y_off) - xdf * u_all
        r_ref[:, lanes] = (xc * u_all).astype(BF)
        carry = ds * last
        moved = fold8(xdf * u_state) + fold8(carry * s_low.astype(F32))
        g_row[0:8, lanes] += fold8(g * xc)
        g_row[8:16, lanes] = moved
        ds_ref[:, lanes] = carry + dotf(ct_low, eg_low)
        du = d_xc * (sig * (1.0 + u * (1.0 - sig)))
        dubuf[0:Q, lanes] = du
        for k in range(CONV):
            g_chan[8 * k : 8 * k + 8, lanes] += fold8(du * xbuf[5 + k : 5 + k + Q, lanes])
        g_chan[8 * CONV : 8 * CONV + 8, lanes] += fold8(du)
        dxdb[:, lanes] = back_conv(dubuf, chan, lanes).astype(BF)
    owner = lax.broadcasted_iota(jnp.int32, (inner, 128), 0) // 64
    spread = (owner == lax.broadcasted_iota(jnp.int32, (inner, 128), 1)).astype(BF)
    qv = q_ref[...]
    q_hi = qv.astype(BF)
    q_lo = (qv - q_hi.astype(F32)).astype(BF)
    q_heads = dotf(q_hi, spread) + dotf(q_lo, spread)
    r_heads = dotf(r_ref[...], spread)
    moved = g_row[8:16, :]
    m_hi = moved.astype(BF)
    m_lo = (moved - m_hi.astype(F32)).astype(BF)
    whole = jnp.sum(dotf(m_hi, spread) + dotf(m_lo, spread), axis=0, keepdims=True)
    rows = lax.broadcasted_iota(jnp.int32, (Q, Q), 0)
    cols = lax.broadcasted_iota(jnp.int32, (Q, Q), 1)
    d_a = dot_exact((rows <= cols).astype(F32), q_heads) + whole
    a_row = -jnp.exp(head[1:2, :])
    d_dt = r_heads + d_a * a_row
    d_raw = d_dt * sigmoid(dt_in + head[0:1, :])
    g_head[0:8, :] += fold8(d_raw)
    g_head[8:16, :] += fold8(d_a * a_row * dt)

    @pl.when(step == blocks - 1)
    def _():
        skip = g_row[0:8, :]
        s_hi = skip.astype(BF)
        s_lo = (skip - s_hi.astype(F32)).astype(BF)
        g_head[16:24, :] = dotf(s_hi, spread) + dotf(s_lo, spread)

    dxdb[:, inner : inner + 128] = d_raw.astype(BF)
    d_scores = (d_scores * tri).astype(BF)
    d_c = d_c + dotf(d_scores, b_low)
    d_b = d_b + dotf(d_scores, c_low, ((0,), (0,)))
    slope = sig_bc * (1.0 + u_bc * (1.0 - sig_bc))
    for lanes, part in ((slice(0, 128), d_b), (slice(128, 256), d_c)):
        du = part * slope[:, lanes]
        dubc[0:Q, lanes] = du
        for k in range(CONV):
            g_state[8 * k : 8 * k + 8, lanes] += fold8(du * bcbuf[5 + k : 5 + k + Q, lanes])
        g_state[8 * CONV : 8 * CONV + 8, lanes] += fold8(du)
    dxdb[:, bc_at : bc_at + 256] = back_conv(dubc, state_p, slice(0, 256)).astype(BF)


MESH=pl.DeviceIdType.MESH
def dp_places(n):
    hi=n//2
    me=lax.axis_index("dp"); mp=lax.axis_index("mp")
    z=me//2; x=me%2
    return hi,z,x,mp


def put(s,d,a,b,dev):
    return pltpu.make_async_remote_copy(s,d,a,b,device_id=dev,device_id_type=MESH)
def add_rows(dst,parts,rows,dtype):
    def body(i,_):
        s=pl.ds(pl.multiple_of(i*16,16),16)
        total=parts[0][s,:].astype(jnp.float32)
        for q in parts[1:]: total=total+q[s,:].astype(jnp.float32)
        dst[s,:]=total.astype(dtype)
        return 0
    lax.fori_loop(0,rows//16,body,0)


def cuts_of(rows, plain=False):
    if plain:
        return [(0, rows)], 0
    if rows < 128:
        return [(0, rows // 2), (rows // 2, rows - rows // 2)], 0
    wide = rows // 8
    part = (rows - wide) // 3 // 16 * 16
    return [(0, wide), (wide, part), (wide + part, part), (wide + 2 * part, rows - wide - 2 * part)], 1


def ag_flow(n, plan, src, out, sems, shard_us, on_shard, begin=0, level_us=None):
    (rs, rr, ls, lr, xs, xr) = sems
    hi, z, x, mp = dp_places(n)
    rows = src.shape[0]
    cuts, wide = plan
    chunks = len(cuts)
    unit = shard_us / rows
    xp, right, left = (z * 2 + 1 - x, mp), ((z + 1) * 2 + x, mp), ((z - 1) * 2 + x, mp)
    hr, hl = z < hi - 1, z > 0
    narrow, wides = list(range(wide, chunks)), list(range(wide))

    def mine(c):
        return src.at[pl.ds(*cuts[c])]

    def at(zz, xx, c):
        return out.at[pl.ds(pl.multiple_of((zz * 2 + xx) * rows + cuts[c][0], 16), cuts[c][1])]

    def zright(t, c, lane, s=None):
        d = at(z + 1 - t, x if lane == 0 else 1 - x, c)
        return put(d if s is None else s, d, rs.at[t, c, lane], rr.at[t, c, lane], right)

    def zleft(t, c, lane, s=None):
        d = at(z - 1 + t, x if lane == 0 else 1 - x, c)
        return put(d if s is None else s, d, ls.at[t, c, lane], lr.at[t, c, lane], left)

    def xsend(slot, zz, c, s=None):
        d = at(zz, x, c)
        return put(d if s is None else s, d, xs.at[slot, c], xr.at[slot, c], xp)

    def xin(slot, zz, c):
        d = at(zz, 1 - x, c)
        put(d, d, xs.at[slot, c], xr.at[slot, c], xp).wait_recv()

    ev = []

    def start():
        for c in wides:
            xsend(0, z, c, mine(c)).start()
        for c in wides + narrow:
            @pl.when(hr)
            def _():
                zright(1, c, 0, mine(c)).start()

            @pl.when(hl)
            def _():
                zleft(1, c, 0, mine(c)).start()
        for c in narrow:
            xsend(0, z, c, mine(c)).start()

    ev.append((begin, start))

    def wide_in(c):
        xin(0, z, c)

        @pl.when(hr)
        def _():
            zright(1, c, 1).start()

        @pl.when(hl)
        def _():
            zleft(1, c, 1).start()

    now = begin + 4
    for c in wides:
        ev.append((now + unit * cuts[c][1], functools.partial(wide_in, c)))

    def hop(t, c, lane, fwd_x):
        xx = x if lane == 0 else 1 - x

        @pl.when(z >= t)
        def _():
            d = at(z - t, xx, c)
            put(d, d, rs.at[t, c, lane], rr.at[t, c, lane], left).wait_recv()
            if t < hi - 1:
                @pl.when(hr)
                def _():
                    zright(t + 1, c, lane).start()
            if fwd_x:
                xsend(t, z - t, c).start()

        @pl.when(z + t <= hi - 1)
        def _():
            d = at(z + t, xx, c)
            put(d, d, ls.at[t, c, lane], lr.at[t, c, lane], right).wait_recv()
            if t < hi - 1:
                @pl.when(hl)
                def _():
                    zleft(t + 1, c, lane).start()
            if fwd_x:
                xsend(hi - 1 + t, z + t, c).start()

    seq = [(c, 0, False) for c in wides] + [(c, 0, True) for c in narrow] + [(c, 1, False) for c in wides]
    level_us = level_us or unit * sum(cuts[c][1] for c, _, _ in seq)
    for t in range(1, hi):
        now = begin + 4 + level_us * (t - 1)
        for c, lane, fwd in seq:
            now = now + unit * cuts[c][1]
            ev.append((now, functools.partial(hop, t, c, lane, fwd)))
    z_end = now
    ev.append((z_end, lambda: on_shard(z, x)))

    def near_shards(t):
        @pl.when(z >= t)
        def _():
            on_shard(z - t, x)

        @pl.when(z + t <= hi - 1)
        def _():
            on_shard(z + t, x)

    for t in range(1, hi):
        ev.append((z_end, functools.partial(near_shards, t)))

    def far_own():
        for c in narrow:
            xin(0, z, c)
        on_shard(z, 1 - x)

    def far(t):
        @pl.when(z >= t)
        def _():
            for c in narrow:
                xin(t, z - t, c)
            on_shard(z - t, 1 - x)

        @pl.when(z + t <= hi - 1)
        def _():
            for c in narrow:
                xin(hi - 1 + t, z + t, c)
            on_shard(z + t, 1 - x)

    ev.append((z_end, far_own))
    for t in range(1, hi):
        ev.append((z_end, functools.partial(far, t)))

    def drain():
        for c in range(chunks):
            xsend(0, z, c, mine(c)).wait_send()
        for t in range(1, hi):
            for c in range(chunks):
                for lane in (0,) if c in narrow else (0, 1):
                    @pl.when(hr & (z + 1 - t >= 0))
                    def _():
                        zright(t, c, lane).wait_send()

                    @pl.when(hl & (z - 1 + t <= hi - 1))
                    def _():
                        zleft(t, c, lane).wait_send()
                if c in narrow:
                    @pl.when(z >= t)
                    def _():
                        xsend(t, z - t, c).wait_send()

                    @pl.when(z + t <= hi - 1)
                    def _():
                        xsend(hi - 1 + t, z + t, c).wait_send()

    return ev, drain


def run_until(events, at, limit):
    while at < len(events) and events[at][0] <= limit:
        events[at][1]()
        at += 1
    return at


def signal_dp(n, bar):
    hi, z, x, mp = dp_places(n)
    pl.semaphore_signal(bar, inc=1, device_id=(z * 2 + 1 - x, mp), device_id_type=MESH)

    @pl.when(z > 0)
    def _():
        pl.semaphore_signal(bar, inc=1, device_id=((z - 1) * 2 + x, mp), device_id_type=MESH)

    @pl.when(z < hi - 1)
    def _():
        pl.semaphore_signal(bar, inc=1, device_id=((z + 1) * 2 + x, mp), device_id_type=MESH)

    return 1 + (z > 0).astype(jnp.int32) + (z < hi - 1).astype(jnp.int32)


def signal_mp(m, bar):
    dp, mp = lax.axis_index("dp"), lax.axis_index("mp")
    for k in range(1, m):
        pl.semaphore_signal(bar, inc=1, device_id=(dp, lax.rem(mp + k, m)), device_id_type=MESH)
    return m - 1


def accumulate(acc, acc_at, lhs, rhs, k_at, k, fresh):
    rows = acc.shape[0]

    def tile(i, _):
        r = pl.ds(pl.multiple_of(i * 256, 256), 256)
        a = lhs[r, pl.ds(k_at, k)]
        for j, step in column_steps(rhs.shape[1]):
            new = dotf(a, rhs[pl.ds(k_at, k), j : j + step])
            cols = slice(acc_at + j, acc_at + j + step)
            acc[r, cols] = new if fresh else acc[r, cols] + new
        return 0

    lax.fori_loop(0, rows // 256, tile, 0)


def front_kernel(
    n, m, plan, inner, blocks,
    gain, chan, state_p, head, hrow, gate, chans, w_dt, w_bc, tokens, cot, w_zx, w_out,
    xdb_out, quant, full_x, full_s, full_z, full_out, states, nout, d_z, d_y, g_gate,
    xbuf, bcbuf, s_ref, y, slope, xdb, wx, ws, wz, wo, zv, dn, qv, cv, wf, of, sb, nb, pb, fb, sums, got,
    lsem, bsem, ss, sr, *sems,
):
    k = pl.program_id(0)
    c = k - 1
    dp, mp = lax.axis_index("dp"), lax.axis_index("mp")
    owned, heads = w_bc.shape[0], w_dt.shape[0]
    rows = y.shape[0]
    fine = owned % 128 == 0
    near = (dp, mp + 1 - 2 * lax.rem(mp, 2))
    far = (dp, lax.rem(mp + 2, 4))
    pair = mp // 2
    even = lax.rem(mp, 2) == 0
    bc_at = inner + 128
    mine = pl.ds(pl.multiple_of(dp * owned, 16), owned)

    def adder(acc, lhs, w):
        def on_shard(zz, xx):
            if fine:
                accumulate(acc, 0, lhs, w, pl.multiple_of((zz * 2 + xx) * owned, owned), owned, False)

        return on_shard

    def whole(acc, lhs, w):
        if not fine:
            accumulate(acc, 0, lhs, w, 0, w.shape[0], True)

    ns = len(sems) // 4
    single = cuts_of(owned, True)
    es, drain_s = ag_flow(n, single, ws.at[mine], ws, sems[:ns], 1.5, lambda zz, xx: None, TF["s"], TF["s_level"])
    ex, drain_x = ag_flow(n, plan, wx.at[mine], wx, sems[ns : 2 * ns], 11.3, adder(xdb, qv, wx), TF["x"])
    ez, drain_z = ag_flow(n, plan, wz.at[mine], wz, sems[2 * ns : 3 * ns], 11.3, adder(zv, qv, wz), TF["z"])
    eo, drain_o = ag_flow(n, plan, wo.at[mine], wo, sems[3 * ns :], 11.3, adder(dn, cv, wo), TF["o"])

    def load(src, dst, i):
        return pltpu.make_async_copy(src, dst, lsem.at[i])

    load_w, load_o, load_t, load_c = load(w_zx, wf, 0), load(w_out, of, 1), load(tokens, cv, 2), load(cot, cv, 3)
    keep_q, keep_x, keep_s = load(qv, quant, 4), load(wx, full_x, 5), load(ws, full_s, 6)
    keep_z, keep_o, keep_d = load(wz, full_z, 7), load(wo, full_out, 8), load(xdb, xdb_out, 9)
    to_near = put(sb, nb, bsem.at[0], bsem.at[1], near)
    to_far = put(pb, fb, bsem.at[2], bsem.at[3], far)

    def cast_part(dst, part):
        lanes = inner // 128

        def tile(i, _):
            at = pl.multiple_of(i * 32 * lanes, 32 * lanes)
            r = pl.ds(pl.multiple_of(dp * owned + i * 16, 16), 16)
            for j in range(lanes):
                v = wf[pl.ds(at + 2 * j + part, 16, stride=2 * lanes), :]
                dst[r, j * 128 : (j + 1) * 128] = v.astype(BF)
            return 0

        lax.fori_loop(0, owned // 16, tile, 0)

    def cast_s():
        block = w_bc[:, pl.ds(pl.multiple_of(pair * 128, 128), 128)]
        v = jnp.where(even, pltpu.roll(block, 64, 1), block)
        steps = jnp.concatenate([w_dt[...], jnp.zeros((128 - heads, owned), F32)], axis=0).T
        ws[mine, :] = jnp.where(lanes_below(owned, 64), steps, v).astype(BF)

    def cast_o():
        load_o.wait()
        wo[mine, :] = of[...].astype(BF)

    def norm(part):
        if part == 0:
            load_t.wait()

        def tile(i, _):
            r = pl.ds(pl.multiple_of(i * 16, 16), 16)
            x = cv[r, :].astype(F32)
            scale = lax.rsqrt(jnp.mean(x * x, axis=-1, keepdims=True) + EPS)
            qv[r, :] = (x * scale * gain[0:1, :]).astype(BF)
            return 0

        per = rows // 64
        lax.fori_loop(part * per, (part + 1) * per, tile, 0)
        if part == 3:
            keep_q.start()
            load_c.start()
            xdb[:, 0:inner] = jnp.zeros((rows, inner), F32)

    def steps_and_states():
        accumulate(sb, 0, qv, ws, 0, ws.shape[0], True)
        to_near.start()
        xdb[:, inner:bc_at] = jnp.where(lanes_below(rows, 64), sb[...], 0.0)

    def pairs():
        to_near.wait_recv()

        def tile(i, _):
            r = pl.ds(pl.multiple_of(i * 128, 128), 128)
            a, b = sb[r, :], nb[r, :]
            one = jnp.where(even, a, b)
            two = jnp.where(even, b, a)
            v = jnp.where(lanes_below(128, 64), pltpu.roll(one, 64, 1), two)
            pb[r, :] = v
            xdb[r, pl.ds(pl.multiple_of(bc_at + pair * 128, 128), 128)] = v
            return 0

        lax.fori_loop(0, rows // 128, tile, 0)
        to_far.start()

    def others():
        to_far.wait_recv()
        xdb[:, pl.ds(pl.multiple_of(bc_at + (1 - pair) * 128, 128), 128)] = fb[...]

    def clear():
        zv[...] = jnp.zeros_like(zv)
        dn[...] = jnp.zeros_like(dn)

    def x_done():
        whole(xdb, qv, wx)
        keep_d.start()
        keep_x.start()
        keep_s.start()

    def rows_at(i):
        return pl.ds(pl.multiple_of(i * 128, 128), 128)

    def gates():
        whole(zv, qv, wz)
        keep_z.start()

        def tile(i, _):
            r = rows_at(i)
            total = jnp.zeros((128, 128), F32)
            for j in range(0, inner, 128):
                lanes = slice(j, j + 128)
                z, yv = zv[r, lanes], y[r, lanes]
                sig = sigmoid(z)
                act = z * sig
                gated = yv * act
                total = total + gated * gated
                slope[r, lanes] = yv * (sig * (1.0 + z * (1.0 - sig)))
                zv[r, lanes] = act * hrow[1:2, lanes]
                y[r, lanes] = gated
            sums[0:1, r] = jnp.sum(total.T, axis=0, keepdims=True)
            return 0

        lax.fori_loop(0, rows // 128, tile, 0)

    def last(events):
        return max(t for t, _ in events)

    x_last = last(ex) + 0.1
    before = ordered_events(
        es[1:], ex[1:], ez, eo,
        [(2 * part + 0.1, functools.partial(norm, part)) for part in range(4)],
        [(TF["cast_z"], functools.partial(cast_part, wz, 0)), (TF["cast_o"], cast_o), (TF["clear"], clear)],
        [(TF["steps"], steps_and_states), (TF["pairs"], pairs), (x_last - 0.05, others), (x_last, x_done)],
    )
    cut = [i for i, e in enumerate(before) if e[1] is x_done][0] + 1
    events = ordered_events(before[cut:], [(last(ez) + TF["gates"], gates)])

    @pl.when(k == 0)
    def _():
        bar = pltpu.get_barrier_semaphore()
        count = signal_dp(n, bar) + signal_mp(m, bar)
        for copy in (load_w, load_t, load_o):
            copy.start()
        cast_s()
        load_w.wait()
        cast_part(wx, 1)
        pl.semaphore_wait(bar, count)
        es[0][1]()
        ex[0][1]()
        for e in before[:cut]:
            e[1]()

    at = 0
    clock = x_last + TF["scan"]
    for i in range(1, blocks + 1):
        end = at
        while end < len(events) and events[end][0] <= clock:
            end += 1
        if end > at:
            @pl.when(k == i)
            def _():
                for e in events[at:end]:
                    e[1]()
        at = end
        clock += TF["step"]
    rest = events[at:]
    assert any(e[1] is gates for e in rest)

    @pl.when((k > 0) & (k <= blocks))
    def _():
        here = pl.ds(pl.multiple_of(c * Q, Q), Q)
        scan_fwd_block(c, inner, xdb.at[here], chan, state_p, head, hrow, y, states, xbuf, bcbuf, s_ref)

    @pl.when(k == blocks + 1)
    def _():
        load_c.wait()
        sums[...] = jnp.zeros_like(sums)
        g_gate[...] = jnp.zeros_like(g_gate)
        for e in rest:
            e[1]()
        whole(dn, cv, wo)
        keep_o.start()
        half = rows // 2

        def tokens_of(h):
            return pl.ds(h * half, half)

        def to_mp(d, h):
            s = tokens_of(h)
            return put(got.at[mp, :, s], got.at[mp, :, s], ss.at[d, h], sr.at[mp, h], (dp, d))

        def from_mp(d, h):
            s = tokens_of(h)
            return put(got.at[d, :, s], got.at[d, :, s], ss.at[d, h], sr.at[d, h], (dp, d))

        def dots(i, _):
            r = rows_at(i)
            total = jnp.zeros((128, 128), F32)
            for j in range(0, inner, 128):
                lanes = slice(j, j + 128)
                total = total + (dn[r, lanes] * gate[0:1, lanes]) * y[r, lanes]
            sums[1:2, r] = jnp.sum(total.T, axis=0, keepdims=True)
            return 0

        per = chans[0:1, 0:1]

        def finish(i, _):
            r = rows_at(i)
            scale = lax.rsqrt(sums[0:1, r] * per + EPS)
            coef = scale * scale * sums[1:2, r] * per
            scale = jnp.broadcast_to(scale, (128, 128)).T
            coef = jnp.broadcast_to(coef, (128, 128)).T
            for j in range(0, inner, 128):
                lanes = slice(j, j + 128)
                gg = gate[0:1, lanes]
                dnv = dn[r, lanes]
                scaled = y[r, lanes] * scale
                nout[r, lanes] = (scaled * gg).astype(BF)
                g_gate[:, lanes] += fold8(scaled * dnv)
                d_gated = dnv * gg * scale - scaled * coef
                d_z[r, lanes] = (d_gated * slope[r, lanes]).astype(BF)
                d_y[r, lanes] = (d_gated * zv[r, lanes]).astype(BF)
            return 0

        mps = [lax.rem(mp + q, m) for q in range(1, m)]
        tiles = half // 128
        for h in range(2):
            lax.fori_loop(h * tiles, (h + 1) * tiles, dots, 0)
            s = slice(h * half, (h + 1) * half)
            got[mp, :, s] = sums[:, s]
            for d in mps:
                to_mp(d, h).start()
        for h in range(2):
            s = slice(h * half, (h + 1) * half)
            for d in mps:
                from_mp(d, h).wait_recv()
            total = got[0, :, s]
            for d in range(1, m):
                total = total + got[d, :, s]
            sums[:, s] = total
            lax.fori_loop(h * tiles, (h + 1) * tiles, finish, 0)
        for h in range(2):
            for d in mps:
                to_mp(d, h).wait_send()
        to_near.wait_send()
        to_far.wait_send()
        for drain in (drain_s, drain_x, drain_z, drain_o):
            drain()
        for copy in (keep_q, keep_x, keep_s, keep_z, keep_o, keep_d):
            copy.wait()


TF = {
    "s": 0, "s_level": 12.7, "x": 0, "z": 20, "o": 58, "cast_z": 9, "cast_o": 10, "clear": 11,
    "steps": 33, "pairs": 37, "scan": 6, "step": 2.4, "gates": 16,
}


def ordered_events(*lists):
    return sorted([e for q in lists for e in q], key=lambda e: e[0])


def front(tokens, cot, gain, chan, state_p, head, hrow, gate, chans, w_zx, w_out, w_dt, w_bc, n, m, cid):
    rows, model = tokens.shape
    inner = chan.shape[1]
    blocks = rows // Q
    owned = w_bc.shape[0]
    full = n * owned
    hi = n // 2
    plan = cuts_of(owned)
    chunks = len(plan[0])
    whole = lambda a: pl.BlockSpec(a.shape, lambda k: (0, 0))
    any_ = pl.BlockSpec(memory_space=pl.ANY)
    D, V = pltpu.SemaphoreType.DMA, pltpu.VMEM
    token = lambda: pl.BlockSpec((rows, inner), lambda k: (0, 0))
    shape = jax.ShapeDtypeStruct
    ones = [D((hi, 1, 2))] * 4 + [D((2 * hi - 1, 1))] * 2
    many = [D((hi, chunks, 2))] * 4 + [D((2 * hi - 1, chunks))] * 2
    return pl.pallas_call(
        functools.partial(front_kernel, n, m, plan, inner, blocks),
        grid=(blocks + 2,),
        in_specs=[whole(a) for a in (gain, chan, state_p, head, hrow, gate, chans, w_dt, w_bc)] + [any_] * 4,
        out_specs=(any_,) * 6
        + (
            pl.BlockSpec((1, 128, inner), lambda k: (jnp.clip(k - 1, 0, blocks - 1), 0, 0)),
            token(), token(), token(),
            pl.BlockSpec((8, inner), lambda k: (0, 0)),
        ),
        out_shape=(
            shape((rows, inner + 384), F32), shape((rows, model), BF),
            shape((full, inner), BF), shape((full, 128), BF), shape((full, inner), BF), shape((full, inner), BF),
            shape((blocks, 128, inner), BF),
            shape((rows, inner), BF), shape((rows, inner), BF), shape((rows, inner), BF),
            shape((8, inner), F32),
        ),
        scratch_shapes=[
            V((Q + 8, inner), F32), V((Q + 8, 256), F32), V((128, inner), F32),
            V((rows, inner), F32), V((rows, inner), F32), V((rows, inner + 384), F32),
            V((full, inner), BF), V((full, 128), BF), V((full, inner), BF), V((full, inner), BF),
            V((rows, inner), F32), V((rows, inner), F32), V((rows, model), BF), V((rows, model), BF),
            V(w_zx.shape, F32), V(w_out.shape, F32),
            V((rows, 128), F32), V((rows, 128), F32), V((rows, 128), F32), V((rows, 128), F32),
            V((8, rows), F32), V((m, 8, rows), F32),
            D((10,)), D((4,)), D((m, 2)), D((m, 2)),
        ]
        + ones + many * 3,
        compiler_params=pltpu.CompilerParams(
            collective_id=cid, has_side_effects=True, vmem_limit_bytes=63 * 2**20
        ),
        name="front",
    )(gain, chan, state_p, head, hrow, gate, chans, w_dt, w_bc, tokens, cot, w_zx, w_out)


def rs_scratch(n, plan, rows, w):
    cuts, wide = plan
    chunks = len(cuts)
    hi = n // 2
    D, V = pltpu.SemaphoreType.DMA, pltpu.VMEM
    wd = max(wide, 1)
    tall = cuts[wide - 1][0] + cuts[wide - 1][1] if wide else 16
    ww = w if wide else 128
    return [
        V((hi, rows, w), BF),
        V((hi - 1, rows, w), BF),
        V((hi - 1, rows, w), BF),
        V((hi - 1, 2, tall, ww), BF),
        V((hi - 1, 2, tall, ww), BF),
        V((3, tall, ww), BF),
        D((hi, chunks)), D((hi, chunks)),
        D((hi - 1, chunks)), D((hi - 1, chunks)), D((hi - 1, chunks)), D((hi - 1, chunks)),
        D((hi - 1, 2, wd)), D((hi - 1, 2, wd)), D((hi - 1, 2, wd)), D((hi - 1, 2, wd)),
        D((2, wd)),
    ]


RS_REFS = 17


def rs_flow(n, plan, g, out, scr, shard_us, make, first_us=8, wide_us=0):
    (RX, ZR, ZL, WR, WL, WX, xs, xr, rs, rr, ls, lr, ws, wr, vs, vr, wx) = scr
    hi, z, x, mp = dp_places(n)
    rows = out.shape[0]
    cuts, wide = plan
    chunks = len(cuts)
    xp, right, left = (z * 2 + 1 - x, mp), ((z + 1) * 2 + x, mp), ((z - 1) * 2 + x, mp)
    hr, hl = z < hi - 1, z > 0
    narrow, wides = range(wide, chunks), range(wide)

    def G(zz, xx, c):
        return g.at[pl.ds(pl.multiple_of((zz * 2 + xx) * rows + cuts[c][0], 16), cuts[c][1])]

    def ch(c):
        return pl.ds(*cuts[c])

    def xcopy(tz, c):
        return put(G(tz, 1 - x, c), RX.at[tz, ch(c)], xs.at[tz, c], xr.at[tz, c], xp)

    def rcopy(tz, t, c):
        return put(RX.at[tz, ch(c)], ZR.at[t - 1, ch(c)], rs.at[t - 1, c], rr.at[t - 1, c], right)

    def lcopy(tz, t, c):
        return put(RX.at[tz, ch(c)], ZL.at[t - 1, ch(c)], ls.at[t - 1, c], lr.at[t - 1, c], left)

    def wcopy(t, lane, c, first):
        s = G(z + t, x if lane == 0 else 1 - x, c) if first else WR.at[t, lane, ch(c)]
        return put(s, WR.at[t - 1, lane, ch(c)], ws.at[t - 1, lane, c], wr.at[t - 1, lane, c], right)

    def vcopy(t, lane, c, first):
        s = G(z - t, x if lane == 0 else 1 - x, c) if first else WL.at[t, lane, ch(c)]
        return put(s, WL.at[t - 1, lane, ch(c)], vs.at[t - 1, lane, c], vr.at[t - 1, lane, c], left)

    def rrecv(t, c):
        d = ZR.at[t, ch(c)]
        return put(d, d, rs.at[t, c], rr.at[t, c], xp)

    def lrecv(t, c):
        d = ZL.at[t, ch(c)]
        return put(d, d, ls.at[t, c], lr.at[t, c], xp)

    def wrecv(t, lane, c):
        d = WR.at[t, lane, ch(c)]
        return put(d, d, ws.at[t, lane, c], wr.at[t, lane, c], xp)

    def vrecv(t, lane, c):
        d = WL.at[t, lane, ch(c)]
        return put(d, d, vs.at[t, lane, c], vr.at[t, lane, c], xp)

    def wxcopy(c):
        return put(WX.at[1, ch(c)], WX.at[2, ch(c)], wx.at[0, c], wx.at[1, c], xp)

    def start(t):
        if t == 0:
            make(z)
            for c in narrow:
                xcopy(z, c).start()
            return

        @pl.when(z + t <= hi - 1)
        def _():
            make(z + t)
            for c in narrow:
                xcopy(z + t, c).start()

        @pl.when(z - t >= 0)
        def _():
            make(z - t)
            for c in narrow:
                xcopy(z - t, c).start()

        for c in wides:
            for lane in (0, 1):
                @pl.when(z == 0)
                def _():
                    wcopy(t, lane, c, True).start()

                @pl.when(z == hi - 1)
                def _():
                    vcopy(t, lane, c, True).start()

    starts = [functools.partial(start, t) for t in range(hi - 1, -1, -1)]
    ev = []


    def wstep(t, c):
        for lane in (0, 1):
            xx = x if lane == 0 else 1 - x

            @pl.when((z + t <= hi - 1) & hl)
            def _():
                wrecv(t, lane, c).wait_recv()
                add_rows(WR.at[t, lane, ch(c)], [G(z + t, xx, c), WR.at[t, lane, ch(c)]], cuts[c][1], BF)
                wcopy(t, lane, c, False).start()

            @pl.when((z - t >= 0) & hr)
            def _():
                vrecv(t, lane, c).wait_recv()
                add_rows(WL.at[t, lane, ch(c)], [G(z - t, xx, c), WL.at[t, lane, ch(c)]], cuts[c][1], BF)
                vcopy(t, lane, c, False).start()

    def wown(c):
        for lane in (1, 0):
            xx = x if lane == 0 else 1 - x
            dst = WX.at[lane, ch(c)]

            @pl.when(hl)
            def _():
                wrecv(0, lane, c).wait_recv()

            @pl.when(hr)
            def _():
                vrecv(0, lane, c).wait_recv()

            @pl.when(hl & hr)
            def _():
                add_rows(dst, [G(z, xx, c), WR.at[0, lane, ch(c)], WL.at[0, lane, ch(c)]], cuts[c][1], BF)

            @pl.when(jnp.logical_not(hr))
            def _():
                add_rows(dst, [G(z, xx, c), WR.at[0, lane, ch(c)]], cuts[c][1], BF)

            @pl.when(jnp.logical_not(hl))
            def _():
                add_rows(dst, [G(z, xx, c), WL.at[0, lane, ch(c)]], cuts[c][1], BF)

            if lane == 1:
                wxcopy(c).start()

    def wlast(c):
        wxcopy(c).wait_recv()
        add_rows(out.at[ch(c)], [WX.at[0, ch(c)], WX.at[2, ch(c)]], cuts[c][1], F32)

    def step(t, c, to_right):
        tz = z + t if to_right else z - t
        inside = (tz <= hi - 1) if to_right else (tz >= 0)
        behind = hl if to_right else hr
        copy, recv, buf = (rcopy, rrecv, ZR) if to_right else (lcopy, lrecv, ZL)

        @pl.when(inside)
        def _():
            dst = RX.at[tz, ch(c)]
            xcopy(tz, c).wait_recv()
            if t < hi - 1:
                @pl.when(behind)
                def _():
                    recv(t, c).wait_recv()
                    add_rows(dst, [G(tz, x, c), dst, buf.at[t, ch(c)]], cuts[c][1], BF)

                @pl.when(jnp.logical_not(behind))
                def _():
                    add_rows(dst, [G(tz, x, c), dst], cuts[c][1], BF)
            else:
                add_rows(dst, [G(tz, x, c), dst], cuts[c][1], BF)
            copy(tz, t, c).start()

    def own(c):
        xcopy(z, c).wait_recv()
        base = [G(z, x, c), RX.at[z, ch(c)]]
        o = out.at[ch(c)]

        @pl.when(hl)
        def _():
            rrecv(0, c).wait_recv()

        @pl.when(hr)
        def _():
            lrecv(0, c).wait_recv()

        @pl.when(hl & hr)
        def _():
            add_rows(o, base + [ZR.at[0, ch(c)], ZL.at[0, ch(c)]], cuts[c][1], F32)

        @pl.when(jnp.logical_not(hr))
        def _():
            add_rows(o, base + [ZR.at[0, ch(c)]], cuts[c][1], F32)

        @pl.when(jnp.logical_not(hl))
        def _():
            add_rows(o, base + [ZL.at[0, ch(c)]], cuts[c][1], F32)

    unit = shard_us / rows
    narrow_rows = sum(cuts[c][1] for c in narrow)
    before = cuts[wide][0]
    slot_us = unit * narrow_rows

    def arrives(slot, c):
        return first_us + slot_us * slot + unit * (cuts[c][0] - before + cuts[c][1])

    for t in range(hi - 1, 0, -1):
        slot = min(hi - 1 - t, 2)
        if t < hi - 1:
            for c in wides:
                ev.append((first_us + slot_us * slot, functools.partial(wstep, t, c)))
        for to_right in (True, False):
            for c in narrow:
                late = 1 if t == 1 and not to_right else 0
                ev.append((arrives(slot + late, c), functools.partial(step, t, c, to_right)))
    for c in wides:
        ev.append((first_us + slot_us * (hi - 1), functools.partial(wown, c)))
    for c in narrow:
        ev.append((arrives(hi - 1, c), functools.partial(own, c)))
    for c in wides:
        ev.append((max(wide_us, arrives(hi - 1, chunks - 1) + 0.1), functools.partial(wlast, c)))

    def drain():
        for t in range(hi - 1, 0, -1):
            for c in narrow:
                @pl.when(z + t <= hi - 1)
                def _():
                    xcopy(z + t, c).wait_send()
                    rcopy(z + t, t, c).wait_send()

                @pl.when(z - t >= 0)
                def _():
                    xcopy(z - t, c).wait_send()
                    lcopy(z - t, t, c).wait_send()
            for c in wides:
                for lane in (0, 1):
                    @pl.when(z + t <= hi - 1)
                    def _():
                        wcopy(t, lane, c, True).wait_send()

                    @pl.when(z - t >= 0)
                    def _():
                        vcopy(t, lane, c, True).wait_send()
        for c in narrow:
            xcopy(z, c).wait_send()

    def drain_wide():
        for c in wides:
            wxcopy(c).wait_send()

    begins = [first_us + slot_us * max(j - 1.5, -1) for j in range(hi)]
    return ev, (drain, drain_wide), [(t, f, 1.8) for t, f in zip(begins, starts)]


def ar_scratch(chunks, rows, w):
    D, V = pltpu.SemaphoreType.DMA, pltpu.VMEM
    return [V((rows // 2, w), BF), V((rows // 2, w), BF)] + [D((chunks,))] * 7


AR_REFS = 9


def ar_flow(chunks, p, out, scr, begin, second_us, make, finish):
    (A, B, s0, r0, s1, r1, s2, r2, s3) = scr
    dp, mp = lax.axis_index("dp"), lax.axis_index("mp")
    near = (dp, mp + 1 - 2 * lax.rem(mp, 2))
    far = (dp, lax.rem(mp + 2, 4))
    half = lax.rem(mp, 2)
    rows = p.shape[0] // 2
    cr = rows // chunks

    def ch(c):
        return pl.ds(c * cr, cr)

    def row(h, c):
        return pl.multiple_of(h * rows + c * cr, cr)

    def at(ref, h, c):
        return ref.at[pl.ds(row(h, c), cr)]

    def c0(c):
        return put(at(p, 1 - half, c), A.at[ch(c)], s0.at[c], r0.at[c], near)

    def c1(c):
        return put(A.at[ch(c)], B.at[ch(c)], s1.at[c], r1.at[c], far)

    def c2(c):
        return put(B.at[ch(c)], at(out, half, c), s2.at[c], r2.at[c], near)

    def keep(c):
        return pltpu.make_async_copy(B.at[ch(c)], at(out, half, c), s3.at[c])

    def start():
        for i in range(chunks):
            c0(i).start()

    def phase(u):
        make(u * rows, rows)

        @pl.when(half != u)
        def _():
            start()

    def first(c):
        c0(c).wait_recv()
        add_rows(A.at[ch(c)], [at(p, half, c), A.at[ch(c)]], cr, BF)
        c1(c).start()

    def second(c):
        c1(c).wait_recv()
        finish(row(half, c), cr, A.at[ch(c)], B.at[ch(c)])
        c2(c).start()
        keep(c).start()

    def only(u, f, c):
        @pl.when(half == u)
        def _():
            f(c)

    ev = []
    for c in range(chunks):
        if make is None:
            ev.append((begin + 0.1 * c, functools.partial(first, c)))
            ev.append((second_us + 46 * (c + 1) / chunks, functools.partial(second, c)))
        else:
            for u in range(2):
                ev.append((begin[u] + 0.1 * c, functools.partial(only, u, first, c)))
                ev.append((second_us[u] + 23 * (c + 1) / chunks, functools.partial(only, u, second, c)))

    def sent():
        for c in range(chunks):
            c0(c).wait_send()

    def drain():
        for c in range(chunks):
            c1(c).wait_send()
            c2(c).wait_send()
            keep(c).wait()

    def arrived():
        for c in range(chunks):
            put(at(out, 1 - half, c), at(out, 1 - half, c), s2.at[c], r2.at[c], near).wait_recv()

    return ev, (start if make is None else phase), sent, drain, arrived


def product_rows(dst, d_at, d_col, lhs, rhs, rows):
    tall = min(256, rows)

    def tile(i, _):
        k = pl.multiple_of(d_at + i * tall, tall)
        a = lhs[:, pl.ds(k, tall)]
        for j, step in column_steps(rhs.shape[1]):
            v = dotf(a, rhs[:, j : j + step], ((0,), (0,)))
            dst[pl.ds(k, tall), d_col + j : d_col + j + step] = v.astype(BF)
        return 0

    lax.fori_loop(0, rows // tall, tile, 0)


def product_cols(dst, d_col, lhs, rhs, extra=None):
    def tile(j, _):
        d = pl.ds(pl.multiple_of(j * 256, 256), 256)
        dst[:, d] = dotf(lhs[...], rhs[d, :], ((1,), (1,))).astype(BF)
        return 0

    lax.fori_loop(0, rhs.shape[0] // 256, tile, 0)


T = {
    "out": 14.77,
    "out_wide": 90,
    "z": 54.99,
    "z_wide": 134.39,
    "x": 82.2,
    "s": 102.94,
    "s_pace": 8.48,
    "first1": 16.56,
    "second1": 27.21,
    "tokens": 17.24,
    "clock": 23.59,
    "x_ready": 80.16,
    "sx": [82.2, 82.3, 86, 86.1],
    "far": 82.4,
    "near": 83.49,
    "upper": 82,
    "lower": 91.42,
    "far1": 70.69,
    "near1": 81.9,
    "pz": 5,
    "step": 4.19,
    "z_own": 10.66,
    "x_own": 10.73,
    "s_sends": 85.04,
    "second_up": 92.95,
    "second_low": 105.46,
}


def back_kernel(
    n, m, plan, archunks, inner, blocks,
    xdb, before, dy, states, chan, state_p, head, hrow, gain,
    quant, cot, nout, d_z, full_out, full_z, full_x, full_s, tokens,
    g_out, g_z, g_x, g_s, block_out, input_grad, g_chan, g_state, g_head, g_row, g_gain,
    xbuf, bcbuf, dubuf, dubc, ds_ref, q_ref, r_ref,
    dxdb, dbv, dtv, dsv, fb, sb, nb, qv, cv, nv, dzv, wv, ws, go, gz, gs, p,
    lsem, bsem, free_dp, free_mp, *scr,
):
    k = pl.program_id(0)
    mp = lax.axis_index("mp")
    dp = lax.axis_index("dp")
    owned = g_out.shape[0]
    rows = tokens.shape[0]
    fine = (2 * owned) % 256 == 0
    half_rows = rows // 2
    half_at = pl.multiple_of(lax.rem(mp, 2) * half_rows, half_rows)
    hi, z, x, _ = dp_places(n)
    near = (dp, mp + 1 - 2 * lax.rem(mp, 2))
    far = (dp, lax.rem(mp + 2, 4))
    pair = mp // 2
    even = lax.rem(mp, 2) == 0
    ours = pl.ds(pl.multiple_of(pair * 128, 128), 128)
    theirs = pl.ds(pl.multiple_of((1 - pair) * 128, 128), 128)
    part = [pl.ds(u * half_rows, half_rows) for u in range(2)]

    def to_far(u):
        return put(dbv.at[part[u], theirs], fb.at[part[u]], bsem.at[0, u], bsem.at[1, u], far)

    def to_near(u):
        return put(sb.at[part[u]], nb.at[part[u]], bsem.at[2, u], bsem.at[3, u], near)

    dxv = nv

    def maker(g, lhs, rhs):
        def make(zz):
            if fine:
                product_rows(g, pl.multiple_of(zz * 2 * owned, 2 * owned), 0, lhs, rhs, 2 * owned)

        return make

    def finish_out(r, count, a, b):
        def tile(i, _):
            s = pl.ds(pl.multiple_of(i * 16, 16), 16)
            xv = cv[pl.ds(pl.multiple_of(r - half_at + i * 16, 16), 16), :]
            total = a[s, :].astype(F32) + b[s, :].astype(F32)
            b[s, :] = (xv.astype(F32) + total).astype(BF)
            return 0

        lax.fori_loop(0, count // 16, tile, 0)

    def finish_in(r, count, a, b):
        def tile(i, _):
            s = pl.ds(pl.multiple_of(i * 16, 16), 16)
            t = pl.multiple_of(r - half_at + i * 16, 16)
            xv = cv[pl.ds(t, 16), :].astype(F32)
            scale = lax.rsqrt(jnp.mean(xv * xv, axis=-1, keepdims=True) + EPS)
            xhat = xv * scale
            total = a[s, :].astype(F32) + b[s, :].astype(F32)
            e = gain[0:1, :] * total
            mean = jnp.mean(e * xhat, axis=-1, keepdims=True)
            b[s, :] = (cv[pl.ds(half_rows + t, 16), :].astype(F32) + scale * (e - xhat * mean)).astype(BF)
            v = xhat * total
            g_gain[...] += v[0:8, :] + v[8:16, :]
            return 0

        lax.fori_loop(0, count // 16, tile, 0)

    def make_in(r, count):
        a, b = dxv[pl.ds(r, count), :], dsv[pl.ds(r, count), :]

        def tile(j, _):
            d = pl.ds(pl.multiple_of(j * 256, 256), 256)
            v = dotf(a, wv[d, :], ((1,), (1,))) + dotf(b, ws[d, :], ((1,), (1,)))
            p[pl.ds(r, count), d] = (p[pl.ds(r, count), d].astype(F32) + v).astype(BF)
            return 0

        lax.fori_loop(0, wv.shape[0] // 256, tile, 0)

    def sum_far(u):
        to_far(u).wait_recv()
        r = part[u]
        sb[r, :] = (dbv[r, ours].astype(F32) + fb[r, :].astype(F32)).astype(BF)
        to_near(u).start()

    def sum_near(u):
        to_near(u).wait_recv()

        def tile(i, _):
            r = pl.ds(pl.multiple_of(i * 128, 128), 128)
            v = sb[r, :].astype(F32) + nb[r, :].astype(F32)
            v = jnp.where(even, pltpu.roll(v, 64, 1), v)
            dsv[r, :] = jnp.where(lanes_below(128, 64), dtv[r, :].astype(F32), v).astype(BF)
            return 0

        tiles = half_rows // 128
        lax.fori_loop(u * tiles, (u + 1) * tiles, tile, 0)

    set_a, rest = scr[:RS_REFS], scr[RS_REFS:]
    set_b, rest = rest[:RS_REFS], rest[RS_REFS:]
    set_s, rest = rest[:RS_REFS], rest[RS_REFS:]
    wides_x, rest = rest[:3], rest[3:]
    sems_x, rest = rest[: RS_REFS - 6], rest[RS_REFS - 6 :]
    ar_a, sems_in = rest[:AR_REFS], rest[AR_REFS:]
    set_x = tuple(set_a[:3]) + tuple(wides_x) + tuple(sems_x)
    ar_b = tuple(ar_a[:2]) + tuple(sems_in)
    eo, drain_o, so = rs_flow(n, plan, go, g_out, set_a, 11.3, maker(go, cv, nv), T["out"], T["out_wide"])
    ez, drain_z, sz = rs_flow(n, plan, gz, g_z, set_b, 11.3, maker(gz, qv, dzv), T["z"], T["z_wide"])
    ex, drain_x, sx = rs_flow(n, plan, go, g_x, set_x, 11.3, maker(go, qv, dxv), T["x"])
    es, drain_s, ss = rs_flow(n, cuts_of(owned, True), gs, g_s, set_s, T["s_pace"], lambda zz: None, T["s"])
    e1, start1, sent1, drain1, arrived1 = ar_flow(archunks, p, block_out, ar_a, T["first1"], T["second1"], None, finish_out)
    e2, start2, sent2, drain2, arrived2 = ar_flow(
        archunks, p, input_grad, ar_b, (T["lower"] + 0.1, T["upper"] + 0.1), (T["second_low"], T["second_up"]), make_in, finish_in
    )

    def load(src, dst, i):
        return pltpu.make_async_copy(src, dst, lsem.at[i])

    load_c, load_n = load(cot, cv, 0), load(nout, nv, 1)
    load_wo, load_q, load_dz = load(full_out, wv, 2), load(quant, qv, 3), load(d_z, dzv, 4)
    load_wz, load_wx, load_ws = load(full_z, wv, 5), load(full_x, wv, 6), load(full_s, ws, 7)
    mine = pl.ds(half_at, half_rows)
    load_t = load(tokens.at[mine], cv.at[pl.ds(0, half_rows)], 8)
    load_g = load(cot.at[mine], cv.at[pl.ds(half_rows, half_rows)], 9)

    def whole_product(g, lhs, rhs):
        if not fine:
            product_rows(g, 0, 0, lhs, rhs, g.shape[0])

    def prologue():
        bar = pltpu.get_barrier_semaphore()
        count = signal_dp(n, bar)
        for d in (near, far):
            pl.semaphore_signal(bar, inc=1, device_id=d, device_id_type=MESH)
        for copy in (load_c, load_n, load_wo, load_q, load_dz, load_ws):
            copy.start()
        g_gain[...] = jnp.zeros_like(g_gain)
        pl.semaphore_wait(bar, count + 2)
        load_c.wait()
        load_n.wait()
        whole_product(go, cv, nv)
        so[0][1]()
        load_wo.wait()
        product_cols(p, 0, nv, wv)
        load_wz.start()
        start1()
        for e in so[1:]:
            e[1]()
        tokens_load()
        z_ready()
        for e in sz:
            e[1]()

    def tokens_load():
        load_t.start()
        load_g.start()

    def z_ready():
        load_q.wait()
        load_dz.wait()
        whole_product(gz, qv, dzv)

    def z_branch():
        sent1()
        load_wz.wait()
        product_cols(p, 0, dzv, wv)
        load_wx.start()

    def tokens_in():
        load_t.wait()
        load_g.wait()

    def next_sums():
        drain1()
        for d in (near, far):
            pl.semaphore_signal(free_mp, inc=1, device_id=d, device_id_type=MESH)

    def next_rows():
        drain_o[0]()
        pl.semaphore_signal(free_dp, inc=1, device_id=(z * 2 + 1 - x, mp), device_id_type=MESH)

        @pl.when(z > 0)
        def _():
            pl.semaphore_signal(free_dp, inc=1, device_id=((z - 1) * 2 + x, mp), device_id_type=MESH)

        @pl.when(z < hi - 1)
        def _():
            pl.semaphore_signal(free_dp, inc=1, device_id=((z + 1) * 2 + x, mp), device_id_type=MESH)

    def input_part(u):
        if u == 1:
            load_wx.wait()
            pl.semaphore_wait(free_mp, 2)
        start2(u)

    def s_sends():
        product_rows(gs, 0, 0, qv, dsv, gs.shape[0])
        for e in ss:
            e[1]()

    def x_ready():
        pl.semaphore_wait(free_dp, 1 + (z > 0).astype(jnp.int32) + (z < hi - 1).astype(jnp.int32))
        whole_product(go, qv, dxv)

    def ordered(*lists):
        return sorted([e for q in lists for e in q], key=lambda e: e[0])

    o_last = max(t for t, f in eo if f.func.__name__ == "own")
    one_last = max(t for t, _ in e1)
    def shift(events, by):
        return [(t + (by if f.func.__name__ in ("own", "wown", "wlast") else 0), f) for t, f in events]

    ez, ex = shift(ez, T["z_own"]), shift(ex, T["x_own"])
    early = ordered(eo, ez, e1, [(T["tokens"], tokens_in), (o_last + 0.1, next_rows), (one_last + 0.1, next_sums)])
    late = [
        (T["x_ready"], x_ready), (T["far"], functools.partial(sum_far, 0)), (T["near"], functools.partial(sum_near, 0)),
        (T["upper"], functools.partial(input_part, 1)), (T["lower"], functools.partial(input_part, 0)),
        (T["s_sends"], s_sends),
    ]
    sx = [(t, *e[1:]) for t, e in zip(T["sx"] + T["sx"][-1:] * len(sx), sx)]
    fixed = {blocks // 2: [functools.partial(lambda u: to_far(u).start(), 1)]}
    fixed.setdefault(T["pz"], []).append(z_branch)
    late += [(T["far1"], functools.partial(sum_far, 1)), (T["near1"], functools.partial(sum_near, 1))]
    pl.when(k == 0)(prologue)
    at = 0
    clock = T["clock"]
    for i in range(blocks):
        end = at
        while end < len(early) and early[end][0] <= clock:
            clock += early[end][2] if len(early[end]) > 2 else 0.2
            end += 1
        for f in fixed.get(i, []):
            pl.when(k == i)(f)
        clock += T["step"] + (6.6 if i == T["pz"] else 0)
        if end > at:
            @pl.when(k == i)
            def _():
                for e in early[at:end]:
                    e[1]()
        at = end

    scan_bwd_kernel(
        inner, blocks, xdb, before, dy, states, chan, state_p, head, hrow,
        dxdb, g_chan, g_state, g_head, g_row,
        xbuf, bcbuf, dubuf, dubc, ds_ref, q_ref, r_ref,
    )
    here = pl.ds(pl.multiple_of((blocks - 1 - k) * Q, Q), Q)
    dxv[here, :] = dxdb[:, 0:inner]
    dtv[here, :] = dxdb[:, inner : inner + 128]
    dbv[here, :] = dxdb[:, inner + 128 :]

    @pl.when(k == blocks - 1)
    def _():
        to_far(0).start()
        load_ws.wait()
        for e in ordered(early[at:], late, ex, sx, es, e2):
            e[1]()
        drain_o[1]()
        for flow in (drain_z, drain_x, drain_s):
            flow[0]()
            flow[1]()
        sent2()
        drain2()
        arrived1()
        arrived2()
        for u in range(2):
            to_far(u).wait_send()
            to_near(u).wait_send()


def back(xdb, dy, states, chan, state_p, head, hrow, gain, quant, cot, nout, d_z, full_out, full_z, full_x, full_s, tokens, n, m, archunks, cid):
    rows, width = xdb.shape
    inner = chan.shape[1]
    model = tokens.shape[1]
    blocks = rows // Q
    full = full_out.shape[0]
    owned = full // n
    plan = cuts_of(owned)
    whole = lambda a: pl.BlockSpec(a.shape, lambda s: (0, 0))
    rev = lambda s: (blocks - 1 - s, 0)
    acc = lambda r, w: pl.BlockSpec((r, w), lambda s: (0, 0))
    any_ = pl.BlockSpec(memory_space=pl.ANY)
    V, D = pltpu.VMEM, pltpu.SemaphoreType.DMA
    set_a = rs_scratch(n, plan, owned, inner)
    ar_a = ar_scratch(archunks, rows, model)
    sums = [(owned, inner)] * 3 + [(owned, 128)]
    smalls = [(8 * CONV + 8, inner), (8 * CONV + 8, 256), (24, 128), (16, inner), (8, model)]
    return pl.pallas_call(
        functools.partial(back_kernel, n, m, plan, archunks, inner, blocks),
        grid=(blocks,),
        in_specs=[
            pl.BlockSpec((Q, width), rev),
            pl.BlockSpec((8, width), lambda s: (jnp.maximum((blocks - 1 - s) * (Q // 8) - 1, 0), 0)),
            pl.BlockSpec((Q, inner), rev),
            pl.BlockSpec((1, 128, inner), lambda s: (blocks - 1 - s, 0, 0)),
            whole(chan), whole(state_p), whole(head), whole(hrow), whole(gain),
        ]
        + [any_] * 9,
        out_specs=tuple(acc(*s) for s in sums) + (any_, any_) + tuple(acc(*s) for s in smalls),
        out_shape=tuple(jax.ShapeDtypeStruct(s, F32) for s in sums)
        + (jax.ShapeDtypeStruct(tokens.shape, BF),) * 2
        + tuple(jax.ShapeDtypeStruct(s, F32) for s in smalls),
        scratch_shapes=[
            V((Q + 8, inner), F32), V((Q + 8, 256), F32), V((Q + 8, inner), F32), V((Q + 8, 256), F32),
            V((128, inner), F32), V((Q, inner), F32), V((Q, inner), BF),
            V((Q, width), BF), V((rows, 256), BF), V((rows, 128), BF), V((rows, 128), BF),
            V((rows, 128), BF), V((rows, 128), BF), V((rows, 128), BF),
            V(quant.shape, BF), V(cot.shape, BF), V(nout.shape, BF), V(d_z.shape, BF),
            V(full_out.shape, BF), V(full_s.shape, BF),
            V((full, inner), BF), V((full, inner), BF), V((full, 128), BF), V(tokens.shape, BF),
            D((10,)), D((4, 2)), pltpu.SemaphoreType.REGULAR, pltpu.SemaphoreType.REGULAR,
        ]
        + set_a
        + rs_scratch(n, plan, owned, inner)
        + rs_scratch(n, cuts_of(owned, True), owned, 128)
        + set_a[3:]
        + ar_a
        + ar_a[2:],
        compiler_params=pltpu.CompilerParams(
            collective_id=cid, has_side_effects=True, vmem_limit_bytes=63 * 2**20
        ),
        name="back",
    )(xdb, xdb, dy, states, chan, state_p, head, hrow, gain, quant, cot, nout, d_z, full_out, full_z, full_x, full_s, tokens)


def adam_step(weight, grad, first, second, rate, shrink):
    first = BETA_FIRST * first + (1.0 - BETA_FIRST) * grad
    second = BETA_SECOND * second + (1.0 - BETA_SECOND) * grad * grad
    fix_first = 1.0 - BETA_FIRST**STEP
    fix_second = 1.0 - BETA_SECOND**STEP
    update = first / fix_first / (jnp.sqrt(second / fix_second) + ADAM_EPS) + shrink * weight
    return (weight - rate * update, first, second)


def column_steps(width, step=512):
    return [(j, min(step, width - j)) for j in range(0, width, step)]


def lanes_below(rows, count):
    return lax.broadcasted_iota(jnp.int32, (rows, 128), 1) < count


def square_rows(ref, width):
    def body(i, acc):
        v = ref[pl.ds(pl.multiple_of(i * 8, 8), 8), 0:width]
        v = v * v
        for k in range(width // 128):
            acc = acc + v[:, k * 128 : (k + 1) * 128]
        return acc

    return lax.fori_loop(0, ref.shape[0] // 8, body, jnp.zeros((8, 128), F32))


def tail_kernel(
    n, m, inner, model,
    gz, go, gx, gs, g_chan, g_gate, g_gain, g_state, g_head,
    vec_out, bc_out, norm_out,
    dbuf, mbuf, bcbuf, vs, vr, bs, br, ts, tr,
):
    dp = lax.axis_index("dp")
    mp = lax.axis_index("mp")
    bar = pltpu.get_barrier_semaphore()
    dps = [lax.rem(dp + k, n) for k in range(1, n)]
    mps = [lax.rem(mp + k, m) for k in range(1, m)]
    for d in dps:
        pl.semaphore_signal(bar, inc=1, device_id=(d, mp), device_id_type=MESH)
    for d in mps:
        pl.semaphore_signal(bar, inc=1, device_id=(dp, d), device_id_type=MESH)
    mine = dbuf.at[dp]
    at_gain = 6 * inner // 128
    at_state = at_gain + model // 128
    at_head = at_state + 10
    at_sq = dbuf.shape[1] - 8

    def rows_of(value, row):
        for j in range(value.shape[1] // 128):
            mine[row + j : row + j + 1, :] = value[:, j * 128 : (j + 1) * 128]

    def folded(ref, i):
        return jnp.sum(ref[8 * i : 8 * i + 8, :], axis=0, keepdims=True)

    for q in range(CONV + 1):
        rows_of(folded(g_chan, q), q * inner // 128)
        rows_of(folded(g_state, q), at_state + 2 * q)
    rows_of(folded(g_gate, 0), (CONV + 1) * inner // 128)
    rows_of(folded(g_gain, 0) * (mp < 2).astype(F32), at_gain)
    for q in range(3):
        mine[at_head + q : at_head + q + 1, :] = folded(g_head, q)
    mine[at_head + 3 : at_sq, :] = jnp.zeros((at_sq - at_head - 3, 128), F32)
    mine[at_sq:, :] = square_rows(gz, inner) + square_rows(go, inner) + square_rows(gx, inner) + square_rows(gs, 128)
    bcbuf[mp] = gs[...]
    pl.semaphore_wait(bar, n + m - 2)

    def to_dp(d):
        return put(dbuf.at[dp], dbuf.at[dp], vs.at[d], vr.at[dp], (d, mp))

    def from_dp(d):
        return put(dbuf.at[d], dbuf.at[d], vs.at[d], vr.at[d], (d, mp))

    def to_mp(buf, d, s, r):
        return put(buf.at[mp], buf.at[mp], s.at[d], r.at[mp], (dp, d))

    def from_mp(buf, d, s, r):
        return put(buf.at[d], buf.at[d], s.at[d], r.at[d], (dp, d))

    for d in dps:
        to_dp(d).start()
    for d in mps:
        to_mp(bcbuf, d, bs, br).start()
    for d in dps:
        from_dp(d).wait_recv()
    total = dbuf[0]
    for d in range(1, n):
        total = total + dbuf[d]
    mbuf[mp] = total
    for d in mps:
        to_mp(mbuf, d, ts, tr).start()
    for d in mps:
        from_mp(bcbuf, d, bs, br).wait_recv()
    below = lanes_below(bc_out.shape[0], 64)
    for q in range(m // 2):
        bc_out[:, q * 128 : (q + 1) * 128] = jnp.where(below, pltpu.roll(bcbuf[2 * q], 64, 1), bcbuf[2 * q + 1])
    for d in mps:
        from_mp(mbuf, d, ts, tr).wait_recv()

    def over_mp(a, b):
        v = mbuf[0, a:b, :]
        for d in range(1, m):
            v = v + mbuf[d, a:b, :]
        return v

    per = inner // 128
    start = model // 128
    vec_out[0:start, :] = over_mp(at_gain, at_state)
    for q in range(6):
        for d in range(m):
            at = start + (q * m + d) * per
            vec_out[at : at + per, :] = mbuf[d, q * per : (q + 1) * per, :]
    end = start + 6 * m * per
    vec_out[end : end + 10, :] = over_mp(at_state, at_head)
    heads = inner // 64
    low = lanes_below(1, heads)
    lines = [jnp.zeros((1, 128), F32), jnp.zeros((1, 128), F32)]
    for q in range(3):
        for d in range(m):
            v = jnp.where(low, mbuf[d, at_head + q : at_head + q + 1, :], 0.0)
            spot = q * heads * m + d * heads
            lines[spot // 128] = lines[spot // 128] + (pltpu.roll(v, spot % 128, 1) if spot % 128 else v)
    vec_out[end + 10 : end + 11, :] = lines[0]
    vec_out[end + 11 : end + 12, :] = lines[1]
    vec_out[end + 12 :, :] = jnp.zeros((vec_out.shape[0] - end - 12, 128), F32)
    squares = over_mp(at_sq, at_sq + 8) + square_rows(vec_out, 128)
    squares = jnp.sum(jnp.sum(squares, axis=1, keepdims=True), axis=0, keepdims=True)
    norm_out[...] = jnp.sqrt(jnp.broadcast_to(squares, (8, 128)))
    for d in dps:
        to_dp(d).wait_send()
    for d in mps:
        to_mp(bcbuf, d, bs, br).wait_send()
        to_mp(mbuf, d, ts, tr).wait_send()


def tail_sums(gz, go, gx, gs, g_chan, g_gate, g_gain, g_state, g_head, n, m, cid):
    V = pl.BlockSpec(memory_space=pltpu.VMEM)
    D = pltpu.SemaphoreType.DMA
    owned, inner = gx.shape
    model = g_gain.shape[1]
    rows = -(-(6 * inner // 128 + model // 128 + 13) // 8) * 8 + 8
    total = -(-(model // 128 + 6 * m * inner // 128 + 12) // 8) * 8
    return pl.pallas_call(
        functools.partial(tail_kernel, n, m, inner, model),
        in_specs=[V] * 9,
        out_specs=(V, V, V),
        out_shape=(
            jax.ShapeDtypeStruct((total, 128), F32),
            jax.ShapeDtypeStruct((owned, 256), F32),
            jax.ShapeDtypeStruct((8, 128), F32),
        ),
        scratch_shapes=[
            pltpu.VMEM((n, rows, 128), F32),
            pltpu.VMEM((m, rows, 128), F32),
            pltpu.VMEM((m, owned, 128), F32),
            D((n,)), D((n,)), D((m,)), D((m,)), D((m,)), D((m,)),
        ],
        compiler_params=pltpu.CompilerParams(
            collective_id=cid, has_side_effects=True, vmem_limit_bytes=62 * 2**20
        ),
        name="tail_sums",
    )(gz, go, gx, gs, g_chan, g_gate, g_gain, g_state, g_head)


def adam_kernel(
    inner, heads, blocks,
    norm, gz, go, gx, gs, gbc, block_in, grad_in,
    wz, mz, vz, wd, md, vd, wb, mb, vb, wo, mo, vo,
    nwz, nmz, nvz, nwd, nmd, nvd, nwb, nmb, nvb, nwo, nmo, nvo, block_out, grad_out,
    flat,
):
    step = pl.program_id(0)
    clip = CLIP / jnp.maximum(norm[0:1, 0:1], CLIP)
    rows = gx.shape[0]
    lanes = inner // 128
    block_out[...] = block_in[...]
    grad_out[...] = grad_in[...]

    def update(g, w, mo_, vo_, outs, where):
        new = adam_step(w, g * clip, mo_, vo_, RATE_MATRIX, DECAY_MATRIX)
        for ref, v in zip(outs, new, strict=True):
            ref[where] = v

    for i in range(rows // 8):
        for j in range(lanes):
            cols = slice(j * 128, (j + 1) * 128)
            at = i * 16 * lanes + 2 * j
            flat[pl.ds(at, 8, stride=2 * lanes), :] = gz[8 * i : 8 * i + 8, cols]
            flat[pl.ds(at + 1, 8, stride=2 * lanes), :] = gx[8 * i : 8 * i + 8, cols]

    def zx(i, _):
        s = pl.ds(pl.multiple_of(i * 64, 64), 64)
        update(flat[s, :], wz[s, :], mz[s, :], vz[s, :], (nwz, nmz, nvz), (s, slice(None)))
        return 0

    lax.fori_loop(0, flat.shape[0] // 64, zx, 0)

    def outer(i, _):
        s = pl.ds(pl.multiple_of(i * 8, 8), 8)
        update(go[s, :], wo[s, :], mo[s, :], vo[s, :], (nwo, nmo, nvo), (s, slice(None)))
        return 0

    lax.fori_loop(0, rows // 8, outer, 0)
    update(gbc[...], wb[...], mb[...], vb[...], (nwb, nmb, nvb), (slice(None), slice(None)))

    @pl.when(step == blocks - 1)
    def _():
        g = gs[...].T[0:heads, :]
        update(g, wd[...], md[...], vd[...], (nwd, nmd, nvd), (slice(None), slice(None)))


def adam(norm, gz, go, gx, gs, gbc, block_out, input_grad, groups):
    owned, inner = gx.shape
    heads = groups[1][0].shape[0]
    step = 32
    args = [norm, gz, go, gx, gs, gbc, block_out, input_grad] + [a for group in groups for a in group]

    def spec(a):
        return pl.BlockSpec((a.shape[0] * step // owned, a.shape[1]), lambda i: (i, 0))

    def whole(a):
        return pl.BlockSpec(a.shape, lambda i: (0, 0))

    states = args[8:]
    specs = [whole(a) if i in (3, 4, 5) else spec(a) for i, a in enumerate(states)]
    moved = (block_out, input_grad)
    return pl.pallas_call(
        functools.partial(adam_kernel, inner, heads, owned // step),
        grid=(owned // step,),
        in_specs=[whole(norm), spec(gz), spec(go), spec(gx), whole(gs), spec(gbc)] + [spec(a) for a in moved] + specs,
        out_specs=tuple(specs) + tuple(spec(a) for a in moved),
        out_shape=tuple(jax.ShapeDtypeStruct(a.shape, F32) for a in states)
        + tuple(jax.ShapeDtypeStruct(a.shape, a.dtype) for a in moved),
        scratch_shapes=[pltpu.VMEM((step * 2 * inner // 128, 128), F32)],
        compiler_params=pltpu.CompilerParams(vmem_limit_bytes=62 * 2**20),
        name="adam",
    )(*args)


def pad_rows(a, rows=8):
    return jnp.concatenate([a, jnp.zeros((rows - a.shape[0], a.shape[1]), a.dtype)], axis=0)


def on_device(
    tokens,
    cotangent,
    seq_level,
    w_zx,
    w_dt,
    w_bc,
    w_out,
    vectors,
    m_zx,
    m_dt,
    m_bc,
    m_out,
    m_vec,
    v_zx,
    v_dt,
    v_bc,
    v_out,
    v_vec,
):
    mp_rank = lax.axis_index("mp")
    mp_count = lax.axis_size("mp")
    dp_count = lax.axis_size("dp")
    row_count, model_dim = tokens.shape
    owned = w_zx.shape[0]
    local_inner = w_zx.shape[2]
    inner = local_inner * mp_count
    local_heads = w_dt.shape[1]
    all_heads = local_heads * mp_count
    head_dim = inner // all_heads
    state_dim = w_bc.shape[1] // 2
    gain_in = vectors[:model_dim]
    chan_all = vectors[model_dim : model_dim + 6 * inner].reshape(6, inner)
    chan_loc = lax.dynamic_slice_in_dim(chan_all, mp_rank * local_inner, local_inner, 1)
    state_start = model_dim + 6 * inner
    state_vec = vectors[state_start : state_start + 10 * state_dim].reshape(5, 2 * state_dim)
    head_start = state_start + 10 * state_dim
    head_all = vectors[head_start : head_start + 3 * all_heads].reshape(3, all_heads)
    head_loc = lax.dynamic_slice_in_dim(head_all, mp_rank * local_heads, local_heads, 1)
    active = jnp.left_shift(jnp.int32(all_heads // 8), seq_level[0])
    head_ids = mp_rank * local_heads + jnp.arange(local_heads)
    head_mask = (head_ids < active).astype(F32)
    mask_row = jnp.repeat(head_mask, head_dim)
    chan8 = pad_rows(chan_loc[:5])
    state8 = pad_rows(state_vec)
    head8 = pad_rows(jnp.pad(head_loc[:2], ((0, 0), (0, 128 - local_heads))))
    hrow8 = pad_rows(jnp.stack([jnp.repeat(head_loc[2], head_dim), mask_row]))
    gain8 = pad_rows(gain_in[None])
    channels = (active * head_dim).astype(F32)
    gate8 = pad_rows(chan_loc[5:6])
    per = jnp.full((8, 128), 1.0, F32) / channels

    def flat(a):
        return jnp.swapaxes(a.reshape(owned, 2, local_inner // 128, 128), 1, 2).reshape(-1, 128)

    xdb, quant, full_x, full_s, full_z, full_out, states, normed_out, d_z, d_y, g_gate = front(
        tokens, cotangent, gain8, chan8, state8, head8, hrow8, gate8, per, flat(w_zx), w_out, w_dt.T, w_bc,
        dp_count, mp_count, 1,
    )
    g_out, g_z, g_x, g_s, block_out, input_grad, g_chan, g_state, g_head, g_row, g_gain = back(
        xdb, d_y, states, chan8, state8, head8, hrow8, gain8, quant, cotangent, normed_out, d_z,
        full_out, full_z, full_x, full_s, tokens, dp_count, mp_count, 4, 3,
    )
    vec, g_bc, norm = tail_sums(
        g_z, g_out, g_x, g_s, g_chan, g_gate, g_gain, g_state, g_head, dp_count, mp_count, 5
    )
    grad_norm = norm[0, 0]

    def unflat(a):
        return jnp.swapaxes(a.reshape(owned, local_inner // 128, 2, 128), 1, 2).reshape(w_zx.shape)

    groups = (
        tuple(flat(a) for a in (w_zx, m_zx, v_zx)),
        (w_dt.T, m_dt.T, v_dt.T),
        (w_bc, m_bc, v_bc),
        (w_out, m_out, v_out),
    )
    *new, block_out, input_grad = adam(norm, g_z, g_out, g_x, g_s, g_bc, block_out, input_grad, groups)
    clip = CLIP / jnp.maximum(grad_norm, CLIP)
    small = vec.reshape(-1)[: vectors.shape[0]]
    new_vec = adam_step(vectors, small * clip, m_vec, v_vec, RATE_VECTOR, 0.0)
    new_zx = (unflat(a) for a in new[:3])
    new_dt = (a.T for a in new[3:6])
    return (block_out, input_grad, grad_norm, *new_zx, *new_dt, *new[6:], *new_vec)


def solution(mesh):
    placed = (
        P("dp", None),
        P("dp", None),
        P("dp"),
        P("dp", None, "mp"),
        P("dp", "mp"),
        P("dp", None),
        P("dp", "mp"),
        P(),
        P("dp", None, "mp"),
        P("dp", "mp"),
        P("dp", None),
        P("dp", "mp"),
        P(),
        P("dp", None, "mp"),
        P("dp", "mp"),
        P("dp", None),
        P("dp", "mp"),
        P(),
    )
    return jax.shard_map(
        on_device,
        mesh=mesh,
        in_specs=placed,
        out_specs=(
            P("dp", None),
            P("dp", None),
            P(),
            P("dp", None, "mp"),
            P("dp", None, "mp"),
            P("dp", None, "mp"),
            P("dp", "mp"),
            P("dp", "mp"),
            P("dp", "mp"),
            P("dp", None),
            P("dp", None),
            P("dp", None),
            P("dp", "mp"),
            P("dp", "mp"),
            P("dp", "mp"),
            P(),
            P(),
            P(),
        ),
        check_vma=False,
    )
```

```python
import functools

import jax
import jax.numpy as jnp
from jax import lax
from jax.experimental import pallas as pl
from jax.experimental.pallas import tpu as pltpu
from jax.sharding import PartitionSpec as P

CONV = 4
STEP = 10


EPS = 1e-05
CLIP = 1.0
BETA_FIRST = 0.9
BETA_SECOND = 0.95
ADAM_EPS = 1e-08
RATE_MATRIX = 0.03
RATE_VECTOR = 0.3
DECAY_MATRIX = 0.1


Q = 128
PAIR = 128
LOG2E = 1.4426950408889634
BF = jnp.bfloat16
F32 = jnp.float32


def dotf(a, b, dims=((1,), (0,))):
    return lax.dot_general(a, b, (dims, ((), ())), preferred_element_type=F32)


def dot_exact(a, b):
    return lax.dot_general(
        a, b, (((1,), (0,)), ((), ())), preferred_element_type=F32, precision=lax.Precision.HIGHEST
    )


def softplus(v):
    return jnp.maximum(v, 0.0) + jnp.log(1.0 + jnp.exp(-jnp.abs(v)))


def sigmoid(v):
    return 1.0 / (1.0 + jnp.exp(-v))


def conv_rows(buf, taps, lanes):
    total = taps[CONV : CONV + 1, lanes]
    for k in range(CONV):
        total = total + taps[k : k + 1, lanes] * buf[5 + k : 5 + k + Q, lanes]
    return total


def steps_of(dt_raw, head):
    dt = softplus(dt_raw + head[0:1, :])
    a2 = -jnp.exp(head[1:2, :]) * dt * LOG2E
    rows = lax.broadcasted_iota(jnp.int32, (Q, Q), 0)
    cols = lax.broadcasted_iota(jnp.int32, (Q, Q), 1)
    tri = (rows >= cols).astype(F32)
    return dt, a2, dot_exact(tri, a2), tri


def pick(col0, col1, first):
    return jnp.where(first, col0, col1)


def scan_fwd_block(c, inner, xdb, chan, state_p, head, hrow, y, states, xbuf, bcbuf, s_ref):
    here = pl.ds(pl.multiple_of(c * Q, Q), Q)
    bc_at = inner + 128

    @pl.when(c == 0)
    def _():
        xbuf[0:8, :] = jnp.zeros((8, inner), F32)
        bcbuf[0:8, :] = jnp.zeros((8, 256), F32)
        s_ref[...] = jnp.zeros_like(s_ref)

    @pl.when(c > 0)
    def _():
        xbuf[0:8, :] = xbuf[Q : Q + 8, :]
        bcbuf[0:8, :] = bcbuf[Q : Q + 8, :]

    xbuf[8:, :] = xdb[:, 0:inner]
    bcbuf[8:, :] = xdb[:, bc_at : bc_at + 256]
    u_bc = conv_rows(bcbuf, state_p, slice(0, 256))
    bc = u_bc * sigmoid(u_bc)
    b_low, c_low = bc[:, :128].astype(BF), bc[:, 128:].astype(BF)
    bt_low = bc[:, :128].T.astype(BF)
    dt, _, cum, tri = steps_of(xdb[:, inner : inner + 128], head)
    cum_t = cum.T
    total = cum[Q - 1 : Q, :]
    grow = jnp.exp2(cum)
    tail = jnp.exp2(total - cum)
    scores = dotf(c_low, b_low, ((1,), (1,))) * tri
    states[0] = s_ref[...].astype(BF)
    first = lax.broadcasted_iota(jnp.int32, (Q, PAIR), 1) < 64
    for p in range(inner // PAIR):
        lanes = slice(p * PAIR, (p + 1) * PAIR)
        h0, h1 = slice(2 * p, 2 * p + 1), slice(2 * p + 1, 2 * p + 2)
        u = conv_rows(xbuf, chan, lanes)
        xc = u * sigmoid(u)
        xd = xc * pick(dt[:, h0], dt[:, h1], first)
        xd_low = xd.astype(BF)
        zero = jnp.zeros_like(xd_low)
        m0 = (jnp.exp2(jnp.minimum(cum[:, h0] - cum_t[h0, :], 0.0)) * scores).astype(BF)
        m1 = (jnp.exp2(jnp.minimum(cum[:, h1] - cum_t[h1, :], 0.0)) * scores).astype(BF)
        out = dotf(m0, jnp.where(first, xd_low, zero)) + dotf(m1, jnp.where(first, zero, xd_low))
        s_in = s_ref[:, lanes]
        out = out + dotf(c_low, s_in.astype(BF)) * pick(grow[:, h0], grow[:, h1], first)
        xt = (xd * pick(tail[:, h0], tail[:, h1], first)).astype(BF)
        last = pick(grow[Q - 1 : Q, h0], grow[Q - 1 : Q, h1], first[0:1, :])
        s_ref[:, lanes] = s_in * last + dotf(bt_low, xt)
        y[here, lanes] = (out + hrow[0:1, lanes] * xc) * hrow[1:2, lanes]


def fold8(v):
    return jnp.sum(v.reshape(Q // 8, 8, v.shape[1]), axis=0)


def back_conv(dbuf, taps, lanes):
    total = taps[CONV - 1 : CONV, lanes] * dbuf[0:Q, lanes]
    for k in range(CONV - 1):
        total = total + taps[k : k + 1, lanes] * dbuf[3 - k : 3 - k + Q, lanes]
    return total


def scan_bwd_kernel(
    inner, blocks, xdb, before, dy, states, chan, state_p, head, hrow,
    dxdb, g_chan, g_state, g_head, g_row,
    xbuf, bcbuf, dubuf, dubc, ds_ref, q_ref, r_ref,
):
    step = pl.program_id(0)
    c = blocks - 1 - step
    bc_at = inner + 128

    @pl.when(step == 0)
    def _():
        dubuf[Q:, :] = jnp.zeros((8, inner), F32)
        dubc[Q:, :] = jnp.zeros((8, 256), F32)
        ds_ref[...] = jnp.zeros_like(ds_ref)
        g_chan[...] = jnp.zeros_like(g_chan)
        g_state[...] = jnp.zeros_like(g_state)
        g_head[...] = jnp.zeros_like(g_head)
        g_row[...] = jnp.zeros_like(g_row)

    @pl.when(step > 0)
    def _():
        dubuf[Q:, :] = dubuf[0:8, :]
        dubc[Q:, :] = dubc[0:8, :]

    keep = (c > 0).astype(F32)
    xbuf[0:8, :] = before[:, 0:inner] * keep
    bcbuf[0:8, :] = before[:, bc_at : bc_at + 256] * keep
    xbuf[8:, :] = xdb[:, 0:inner]
    bcbuf[8:, :] = xdb[:, bc_at : bc_at + 256]
    u_bc = conv_rows(bcbuf, state_p, slice(0, 256))
    sig_bc = sigmoid(u_bc)
    bc = u_bc * sig_bc
    b_low, c_low = bc[:, :128].astype(BF), bc[:, 128:].astype(BF)
    ct_low = bc[:, 128:].T.astype(BF)
    dt_in = xdb[:, inner : inner + 128]
    dt, a2, cum, tri = steps_of(dt_in, head)
    cum_t = cum.T
    total = cum[Q - 1 : Q, :]
    grow = jnp.exp2(cum)
    tail = jnp.exp2(total - cum)
    scores = dotf(c_low, b_low, ((1,), (1,))) * tri
    first = lax.broadcasted_iota(jnp.int32, (Q, PAIR), 1) < 64
    d_scores = jnp.zeros((Q, Q), F32)
    d_c = jnp.zeros((Q, 128), F32)
    d_b = jnp.zeros((Q, 128), F32)
    for p in range(inner // PAIR):
        lanes = slice(p * PAIR, (p + 1) * PAIR)
        h0, h1 = slice(2 * p, 2 * p + 1), slice(2 * p + 1, 2 * p + 2)
        u = conv_rows(xbuf, chan, lanes)
        sig = sigmoid(u)
        xc = u * sig
        dte = pick(dt[:, h0], dt[:, h1], first)
        xd = xc * dte
        xd_low = xd.astype(BF)
        zero = jnp.zeros_like(xd_low)
        x0, x1 = jnp.where(first, xd_low, zero), jnp.where(first, zero, xd_low)
        g_low = dy[:, lanes]
        g = g_low.astype(F32)
        g0, g1 = jnp.where(first, g_low, zero), jnp.where(first, zero, g_low)
        l0 = jnp.exp2(jnp.minimum(cum[:, h0] - cum_t[h0, :], 0.0))
        l1 = jnp.exp2(jnp.minimum(cum[:, h1] - cum_t[h1, :], 0.0))
        m0, m1 = (l0 * scores).astype(BF), (l1 * scores).astype(BF)
        d_scores = d_scores + l0 * dotf(g0, xd_low, ((1,), (1,))) + l1 * dotf(g1, xd_low, ((1,), (1,)))
        y_diag = dotf(m0, x0) + dotf(m1, x1)
        u_diag = dotf(m0, g0, ((0,), (0,))) + dotf(m1, g1, ((0,), (0,)))
        grow_e = pick(grow[:, h0], grow[:, h1], first)
        tail_e = pick(tail[:, h0], tail[:, h1], first)
        last = grow_e[Q - 1 : Q, :]
        s_low = states[0, :, lanes]
        ds = ds_ref[:, lanes]
        ds_low = ds.astype(BF)
        eg_low = (g * grow_e).astype(BF)
        y_off = dotf(c_low, s_low) * grow_e
        d_c = d_c + dotf(eg_low, s_low, ((1,), (1,)))
        u_state = dotf(b_low, ds_low) * tail_e
        xt_low = (xd * tail_e).astype(BF)
        d_b = d_b + dotf(xt_low, ds_low, ((1,), (1,)))
        u_all = u_diag + u_state
        xdf = xd_low.astype(F32)
        d_xc = dte * u_all + hrow[0:1, lanes] * g
        q_ref[:, lanes] = g * (y_diag + y_off) - xdf * u_all
        r_ref[:, lanes] = (xc * u_all).astype(BF)
        carry = ds * last
        moved = fold8(xdf * u_state) + fold8(carry * s_low.astype(F32))
        g_row[0:8, lanes] += fold8(g * xc)
        g_row[8:16, lanes] = moved
        ds_ref[:, lanes] = carry + dotf(ct_low, eg_low)
        du = d_xc * (sig * (1.0 + u * (1.0 - sig)))
        dubuf[0:Q, lanes] = du
        for k in range(CONV):
            g_chan[8 * k : 8 * k + 8, lanes] += fold8(du * xbuf[5 + k : 5 + k + Q, lanes])
        g_chan[8 * CONV : 8 * CONV + 8, lanes] += fold8(du)
        dxdb[:, lanes] = back_conv(dubuf, chan, lanes).astype(BF)
    owner = lax.broadcasted_iota(jnp.int32, (inner, 128), 0) // 64
    spread = (owner == lax.broadcasted_iota(jnp.int32, (inner, 128), 1)).astype(BF)
    qv = q_ref[...]
    q_hi = qv.astype(BF)
    q_lo = (qv - q_hi.astype(F32)).astype(BF)
    q_heads = dotf(q_hi, spread) + dotf(q_lo, spread)
    r_heads = dotf(r_ref[...], spread)
    moved = g_row[8:16, :]
    m_hi = moved.astype(BF)
    m_lo = (moved - m_hi.astype(F32)).astype(BF)
    whole = jnp.sum(dotf(m_hi, spread) + dotf(m_lo, spread), axis=0, keepdims=True)
    rows = lax.broadcasted_iota(jnp.int32, (Q, Q), 0)
    cols = lax.broadcasted_iota(jnp.int32, (Q, Q), 1)
    d_a = dot_exact((rows <= cols).astype(F32), q_heads) + whole
    a_row = -jnp.exp(head[1:2, :])
    d_dt = r_heads + d_a * a_row
    d_raw = d_dt * sigmoid(dt_in + head[0:1, :])
    g_head[0:8, :] += fold8(d_raw)
    g_head[8:16, :] += fold8(d_a * a_row * dt)

    @pl.when(step == blocks - 1)
    def _():
        skip = g_row[0:8, :]
        s_hi = skip.astype(BF)
        s_lo = (skip - s_hi.astype(F32)).astype(BF)
        g_head[16:24, :] = dotf(s_hi, spread) + dotf(s_lo, spread)

    dxdb[:, inner : inner + 128] = d_raw.astype(BF)
    d_scores = (d_scores * tri).astype(BF)
    d_c = d_c + dotf(d_scores, b_low)
    d_b = d_b + dotf(d_scores, c_low, ((0,), (0,)))
    slope = sig_bc * (1.0 + u_bc * (1.0 - sig_bc))
    for lanes, part in ((slice(0, 128), d_b), (slice(128, 256), d_c)):
        du = part * slope[:, lanes]
        dubc[0:Q, lanes] = du
        for k in range(CONV):
            g_state[8 * k : 8 * k + 8, lanes] += fold8(du * bcbuf[5 + k : 5 + k + Q, lanes])
        g_state[8 * CONV : 8 * CONV + 8, lanes] += fold8(du)
    dxdb[:, bc_at : bc_at + 256] = back_conv(dubc, state_p, slice(0, 256)).astype(BF)


MESH=pl.DeviceIdType.MESH
def dp_places(n):
    hi=n//2
    me=lax.axis_index("dp"); mp=lax.axis_index("mp")
    z=me//2; x=me%2
    return hi,z,x,mp


def put(s,d,a,b,dev):
    return pltpu.make_async_remote_copy(s,d,a,b,device_id=dev,device_id_type=MESH)
def add_rows(dst,parts,rows,dtype):
    def body(i,_):
        s=pl.ds(pl.multiple_of(i*16,16),16)
        total=parts[0][s,:].astype(jnp.float32)
        for q in parts[1:]: total=total+q[s,:].astype(jnp.float32)
        dst[s,:]=total.astype(dtype)
        return 0
    lax.fori_loop(0,rows//16,body,0)


def cuts_of(rows, plain=False):
    if plain:
        return [(0, rows)], 0
    if rows < 128:
        return [(0, rows // 2), (rows // 2, rows - rows // 2)], 0
    wide = rows // 8
    part = (rows - wide) // 3 // 16 * 16
    return [(0, wide), (wide, part), (wide + part, part), (wide + 2 * part, rows - wide - 2 * part)], 1


def ag_flow(n, plan, src, out, sems, shard_us, on_shard, begin=0, level_us=None):
    (rs, rr, ls, lr, xs, xr) = sems
    hi, z, x, mp = dp_places(n)
    rows = src.shape[0]
    cuts, wide = plan
    chunks = len(cuts)
    unit = shard_us / rows
    xp, right, left = (z * 2 + 1 - x, mp), ((z + 1) * 2 + x, mp), ((z - 1) * 2 + x, mp)
    hr, hl = z < hi - 1, z > 0
    narrow, wides = list(range(wide, chunks)), list(range(wide))

    def mine(c):
        return src.at[pl.ds(*cuts[c])]

    def at(zz, xx, c):
        return out.at[pl.ds(pl.multiple_of((zz * 2 + xx) * rows + cuts[c][0], 16), cuts[c][1])]

    def zright(t, c, lane, s=None):
        d = at(z + 1 - t, x if lane == 0 else 1 - x, c)
        return put(d if s is None else s, d, rs.at[t, c, lane], rr.at[t, c, lane], right)

    def zleft(t, c, lane, s=None):
        d = at(z - 1 + t, x if lane == 0 else 1 - x, c)
        return put(d if s is None else s, d, ls.at[t, c, lane], lr.at[t, c, lane], left)

    def xsend(slot, zz, c, s=None):
        d = at(zz, x, c)
        return put(d if s is None else s, d, xs.at[slot, c], xr.at[slot, c], xp)

    def xin(slot, zz, c):
        d = at(zz, 1 - x, c)
        put(d, d, xs.at[slot, c], xr.at[slot, c], xp).wait_recv()

    ev = []

    def start():
        for c in wides:
            xsend(0, z, c, mine(c)).start()
        for c in wides + narrow:
            @pl.when(hr)
            def _():
                zright(1, c, 0, mine(c)).start()

            @pl.when(hl)
            def _():
                zleft(1, c, 0, mine(c)).start()
        for c in narrow:
            xsend(0, z, c, mine(c)).start()

    ev.append((begin, start))

    def wide_in(c):
        xin(0, z, c)

        @pl.when(hr)
        def _():
            zright(1, c, 1).start()

        @pl.when(hl)
        def _():
            zleft(1, c, 1).start()

    now = begin + 4
    for c in wides:
        ev.append((now + unit * cuts[c][1], functools.partial(wide_in, c)))

    def hop(t, c, lane, fwd_x):
        xx = x if lane == 0 else 1 - x

        @pl.when(z >= t)
        def _():
            d = at(z - t, xx, c)
            put(d, d, rs.at[t, c, lane], rr.at[t, c, lane], left).wait_recv()
            if t < hi - 1:
                @pl.when(hr)
                def _():
                    zright(t + 1, c, lane).start()
            if fwd_x:
                xsend(t, z - t, c).start()

        @pl.when(z + t <= hi - 1)
        def _():
            d = at(z + t, xx, c)
            put(d, d, ls.at[t, c, lane], lr.at[t, c, lane], right).wait_recv()
            if t < hi - 1:
                @pl.when(hl)
                def _():
                    zleft(t + 1, c, lane).start()
            if fwd_x:
                xsend(hi - 1 + t, z + t, c).start()

    seq = [(c, 0, False) for c in wides] + [(c, 0, True) for c in narrow] + [(c, 1, False) for c in wides]
    level_us = level_us or unit * sum(cuts[c][1] for c, _, _ in seq)
    for t in range(1, hi):
        now = begin + 4 + level_us * (t - 1)
        for c, lane, fwd in seq:
            now = now + unit * cuts[c][1]
            ev.append((now, functools.partial(hop, t, c, lane, fwd)))
    z_end = now
    ev.append((z_end, lambda: on_shard(z, x)))

    def near_shards(t):
        @pl.when(z >= t)
        def _():
            on_shard(z - t, x)

        @pl.when(z + t <= hi - 1)
        def _():
            on_shard(z + t, x)

    for t in range(1, hi):
        ev.append((z_end, functools.partial(near_shards, t)))

    def far_own():
        for c in narrow:
            xin(0, z, c)
        on_shard(z, 1 - x)

    def far(t):
        @pl.when(z >= t)
        def _():
            for c in narrow:
                xin(t, z - t, c)
            on_shard(z - t, 1 - x)

        @pl.when(z + t <= hi - 1)
        def _():
            for c in narrow:
                xin(hi - 1 + t, z + t, c)
            on_shard(z + t, 1 - x)

    ev.append((z_end, far_own))
    for t in range(1, hi):
        ev.append((z_end, functools.partial(far, t)))

    def drain():
        for c in range(chunks):
            xsend(0, z, c, mine(c)).wait_send()
        for t in range(1, hi):
            for c in range(chunks):
                for lane in (0,) if c in narrow else (0, 1):
                    @pl.when(hr & (z + 1 - t >= 0))
                    def _():
                        zright(t, c, lane).wait_send()

                    @pl.when(hl & (z - 1 + t <= hi - 1))
                    def _():
                        zleft(t, c, lane).wait_send()
                if c in narrow:
                    @pl.when(z >= t)
                    def _():
                        xsend(t, z - t, c).wait_send()

                    @pl.when(z + t <= hi - 1)
                    def _():
                        xsend(hi - 1 + t, z + t, c).wait_send()

    return ev, drain


def run_until(events, at, limit):
    while at < len(events) and events[at][0] <= limit:
        events[at][1]()
        at += 1
    return at


def signal_dp(n, bar):
    hi, z, x, mp = dp_places(n)
    pl.semaphore_signal(bar, inc=1, device_id=(z * 2 + 1 - x, mp), device_id_type=MESH)

    @pl.when(z > 0)
    def _():
        pl.semaphore_signal(bar, inc=1, device_id=((z - 1) * 2 + x, mp), device_id_type=MESH)

    @pl.when(z < hi - 1)
    def _():
        pl.semaphore_signal(bar, inc=1, device_id=((z + 1) * 2 + x, mp), device_id_type=MESH)

    return 1 + (z > 0).astype(jnp.int32) + (z < hi - 1).astype(jnp.int32)


def signal_mp(m, bar):
    dp, mp = lax.axis_index("dp"), lax.axis_index("mp")
    for k in range(1, m):
        pl.semaphore_signal(bar, inc=1, device_id=(dp, lax.rem(mp + k, m)), device_id_type=MESH)
    return m - 1


def accumulate(acc, acc_at, lhs, rhs, k_at, k, fresh):
    rows = acc.shape[0]

    def tile(i, _):
        r = pl.ds(pl.multiple_of(i * 256, 256), 256)
        a = lhs[r, pl.ds(k_at, k)]
        for j, step in column_steps(rhs.shape[1]):
            new = dotf(a, rhs[pl.ds(k_at, k), j : j + step])
            cols = slice(acc_at + j, acc_at + j + step)
            acc[r, cols] = new if fresh else acc[r, cols] + new
        return 0

    lax.fori_loop(0, rows // 256, tile, 0)


def front_kernel(
    n, m, plan, inner, blocks,
    gain, chan, state_p, head, hrow, gate, chans, w_dt, w_bc, tokens, cot, w_zx, w_out,
    xdb_out, quant, full_x, full_s, full_z, full_out, states, nout, d_z, d_y, g_gate,
    xbuf, bcbuf, s_ref, y, slope, xdb, wx, ws, wz, wo, zv, dn, qv, cv, wf, of, sb, nb, pb, fb, sums, got,
    lsem, bsem, ss, sr, *sems,
):
    k = pl.program_id(0)
    c = k - 1
    dp, mp = lax.axis_index("dp"), lax.axis_index("mp")
    owned, heads = w_bc.shape[0], w_dt.shape[0]
    rows = y.shape[0]
    fine = owned % 128 == 0
    near = (dp, mp + 1 - 2 * lax.rem(mp, 2))
    far = (dp, lax.rem(mp + 2, 4))
    pair = mp // 2
    even = lax.rem(mp, 2) == 0
    bc_at = inner + 128
    mine = pl.ds(pl.multiple_of(dp * owned, 16), owned)

    def adder(acc, lhs, w):
        def on_shard(zz, xx):
            if fine:
                accumulate(acc, 0, lhs, w, pl.multiple_of((zz * 2 + xx) * owned, owned), owned, False)

        return on_shard

    def whole(acc, lhs, w):
        if not fine:
            accumulate(acc, 0, lhs, w, 0, w.shape[0], True)

    ns = len(sems) // 4
    single = cuts_of(owned, True)
    es, drain_s = ag_flow(n, single, ws.at[mine], ws, sems[:ns], 1.5, lambda zz, xx: None, TF["s"], TF["s_level"])
    ex, drain_x = ag_flow(n, plan, wx.at[mine], wx, sems[ns : 2 * ns], 11.3, adder(xdb, qv, wx), TF["x"])
    ez, drain_z = ag_flow(n, plan, wz.at[mine], wz, sems[2 * ns : 3 * ns], 11.3, adder(zv, qv, wz), TF["z"])
    eo, drain_o = ag_flow(n, plan, wo.at[mine], wo, sems[3 * ns :], 11.3, adder(dn, cv, wo), TF["o"])

    def load(src, dst, i):
        return pltpu.make_async_copy(src, dst, lsem.at[i])

    load_w, load_o, load_t, load_c = load(w_zx, wf, 0), load(w_out, of, 1), load(tokens, cv, 2), load(cot, cv, 3)
    keep_q, keep_x, keep_s = load(qv, quant, 4), load(wx, full_x, 5), load(ws, full_s, 6)
    keep_z, keep_o, keep_d = load(wz, full_z, 7), load(wo, full_out, 8), load(xdb, xdb_out, 9)
    to_near = put(sb, nb, bsem.at[0], bsem.at[1], near)
    to_far = put(pb, fb, bsem.at[2], bsem.at[3], far)

    def cast_part(dst, part):
        lanes = inner // 128

        def tile(i, _):
            at = pl.multiple_of(i * 32 * lanes, 32 * lanes)
            r = pl.ds(pl.multiple_of(dp * owned + i * 16, 16), 16)
            for j in range(lanes):
                v = wf[pl.ds(at + 2 * j + part, 16, stride=2 * lanes), :]
                dst[r, j * 128 : (j + 1) * 128] = v.astype(BF)
            return 0

        lax.fori_loop(0, owned // 16, tile, 0)

    def cast_s():
        block = w_bc[:, pl.ds(pl.multiple_of(pair * 128, 128), 128)]
        v = jnp.where(even, pltpu.roll(block, 64, 1), block)
        steps = jnp.concatenate([w_dt[...], jnp.zeros((128 - heads, owned), F32)], axis=0).T
        ws[mine, :] = jnp.where(lanes_below(owned, 64), steps, v).astype(BF)

    def cast_o():
        load_o.wait()
        wo[mine, :] = of[...].astype(BF)

    def norm(part):
        if part == 0:
            load_t.wait()

        def tile(i, _):
            r = pl.ds(pl.multiple_of(i * 16, 16), 16)
            x = cv[r, :].astype(F32)
            scale = lax.rsqrt(jnp.mean(x * x, axis=-1, keepdims=True) + EPS)
            qv[r, :] = (x * scale * gain[0:1, :]).astype(BF)
            return 0

        per = rows // 64
        lax.fori_loop(part * per, (part + 1) * per, tile, 0)
        if part == 3:
            keep_q.start()
            load_c.start()
            xdb[:, 0:inner] = jnp.zeros((rows, inner), F32)

    def steps_and_states():
        accumulate(sb, 0, qv, ws, 0, ws.shape[0], True)
        to_near.start()
        xdb[:, inner:bc_at] = jnp.where(lanes_below(rows, 64), sb[...], 0.0)

    def pairs():
        to_near.wait_recv()

        def tile(i, _):
            r = pl.ds(pl.multiple_of(i * 128, 128), 128)
            a, b = sb[r, :], nb[r, :]
            one = jnp.where(even, a, b)
            two = jnp.where(even, b, a)
            v = jnp.where(lanes_below(128, 64), pltpu.roll(one, 64, 1), two)
            pb[r, :] = v
            xdb[r, pl.ds(pl.multiple_of(bc_at + pair * 128, 128), 128)] = v
            return 0

        lax.fori_loop(0, rows // 128, tile, 0)
        to_far.start()

    def others():
        to_far.wait_recv()
        xdb[:, pl.ds(pl.multiple_of(bc_at + (1 - pair) * 128, 128), 128)] = fb[...]

    def clear():
        zv[...] = jnp.zeros_like(zv)
        dn[...] = jnp.zeros_like(dn)

    def x_done():
        whole(xdb, qv, wx)
        keep_d.start()
        keep_x.start()
        keep_s.start()

    def rows_at(i):
        return pl.ds(pl.multiple_of(i * 128, 128), 128)

    def gates():
        whole(zv, qv, wz)
        keep_z.start()

        def tile(i, _):
            r = rows_at(i)
            total = jnp.zeros((128, 128), F32)
            for j in range(0, inner, 128):
                lanes = slice(j, j + 128)
                z, yv = zv[r, lanes], y[r, lanes]
                sig = sigmoid(z)
                act = z * sig
                gated = yv * act
                total = total + gated * gated
                slope[r, lanes] = yv * (sig * (1.0 + z * (1.0 - sig)))
                zv[r, lanes] = act * hrow[1:2, lanes]
                y[r, lanes] = gated
            sums[0:1, r] = jnp.sum(total.T, axis=0, keepdims=True)
            return 0

        lax.fori_loop(0, rows // 128, tile, 0)

    def last(events):
        return max(t for t, _ in events)

    x_last = last(ex) + 0.1
    before = ordered_events(
        es[1:], ex[1:], ez, eo,
        [(2 * part + 0.1, functools.partial(norm, part)) for part in range(4)],
        [(TF["cast_z"], functools.partial(cast_part, wz, 0)), (TF["cast_o"], cast_o), (TF["clear"], clear)],
        [(TF["steps"], steps_and_states), (TF["pairs"], pairs), (x_last - 0.05, others), (x_last, x_done)],
    )
    cut = [i for i, e in enumerate(before) if e[1] is x_done][0] + 1
    events = ordered_events(before[cut:], [(last(ez) + TF["gates"], gates)])

    @pl.when(k == 0)
    def _():
        bar = pltpu.get_barrier_semaphore()
        count = signal_dp(n, bar) + signal_mp(m, bar)
        for copy in (load_w, load_t, load_o):
            copy.start()
        cast_s()
        load_w.wait()
        cast_part(wx, 1)
        pl.semaphore_wait(bar, count)
        es[0][1]()
        ex[0][1]()
        for e in before[:cut]:
            e[1]()

    at = 0
    clock = x_last + TF["scan"]
    for i in range(1, blocks + 1):
        end = at
        while end < len(events) and events[end][0] <= clock:
            end += 1
        if end > at:
            @pl.when(k == i)
            def _():
                for e in events[at:end]:
                    e[1]()
        at = end
        clock += TF["step"]
    rest = events[at:]
    assert any(e[1] is gates for e in rest)

    @pl.when((k > 0) & (k <= blocks))
    def _():
        here = pl.ds(pl.multiple_of(c * Q, Q), Q)
        scan_fwd_block(c, inner, xdb.at[here], chan, state_p, head, hrow, y, states, xbuf, bcbuf, s_ref)

    @pl.when(k == blocks + 1)
    def _():
        load_c.wait()
        sums[...] = jnp.zeros_like(sums)
        g_gate[...] = jnp.zeros_like(g_gate)
        for e in rest:
            e[1]()
        whole(dn, cv, wo)
        keep_o.start()
        half = rows // 2

        def tokens_of(h):
            return pl.ds(h * half, half)

        def to_mp(d, h):
            s = tokens_of(h)
            return put(got.at[mp, :, s], got.at[mp, :, s], ss.at[d, h], sr.at[mp, h], (dp, d))

        def from_mp(d, h):
            s = tokens_of(h)
            return put(got.at[d, :, s], got.at[d, :, s], ss.at[d, h], sr.at[d, h], (dp, d))

        def dots(i, _):
            r = rows_at(i)
            total = jnp.zeros((128, 128), F32)
            for j in range(0, inner, 128):
                lanes = slice(j, j + 128)
                total = total + (dn[r, lanes] * gate[0:1, lanes]) * y[r, lanes]
            sums[1:2, r] = jnp.sum(total.T, axis=0, keepdims=True)
            return 0

        per = chans[0:1, 0:1]

        def finish(i, _):
            r = rows_at(i)
            scale = lax.rsqrt(sums[0:1, r] * per + EPS)
            coef = scale * scale * sums[1:2, r] * per
            scale = jnp.broadcast_to(scale, (128, 128)).T
            coef = jnp.broadcast_to(coef, (128, 128)).T
            for j in range(0, inner, 128):
                lanes = slice(j, j + 128)
                gg = gate[0:1, lanes]
                dnv = dn[r, lanes]
                scaled = y[r, lanes] * scale
                nout[r, lanes] = (scaled * gg).astype(BF)
                g_gate[:, lanes] += fold8(scaled * dnv)
                d_gated = dnv * gg * scale - scaled * coef
                d_z[r, lanes] = (d_gated * slope[r, lanes]).astype(BF)
                d_y[r, lanes] = (d_gated * zv[r, lanes]).astype(BF)
            return 0

        mps = [lax.rem(mp + q, m) for q in range(1, m)]
        tiles = half // 128
        for h in range(2):
            lax.fori_loop(h * tiles, (h + 1) * tiles, dots, 0)
            s = slice(h * half, (h + 1) * half)
            got[mp, :, s] = sums[:, s]
            for d in mps:
                to_mp(d, h).start()
        for h in range(2):
            s = slice(h * half, (h + 1) * half)
            for d in mps:
                from_mp(d, h).wait_recv()
            total = got[0, :, s]
            for d in range(1, m):
                total = total + got[d, :, s]
            sums[:, s] = total
            lax.fori_loop(h * tiles, (h + 1) * tiles, finish, 0)
        for h in range(2):
            for d in mps:
                to_mp(d, h).wait_send()
        to_near.wait_send()
        to_far.wait_send()
        for drain in (drain_s, drain_x, drain_z, drain_o):
            drain()
        for copy in (keep_q, keep_x, keep_s, keep_z, keep_o, keep_d):
            copy.wait()


TF = {
    "s": 0, "s_level": 12.7, "x": 0, "z": 20, "o": 58, "cast_z": 9, "cast_o": 10, "clear": 11,
    "steps": 33, "pairs": 37, "scan": 6, "step": 2.4, "gates": 16,
}


def ordered_events(*lists):
    return sorted([e for q in lists for e in q], key=lambda e: e[0])


def front(tokens, cot, gain, chan, state_p, head, hrow, gate, chans, w_zx, w_out, w_dt, w_bc, n, m, cid):
    rows, model = tokens.shape
    inner = chan.shape[1]
    blocks = rows // Q
    owned = w_bc.shape[0]
    full = n * owned
    hi = n // 2
    plan = cuts_of(owned)
    chunks = len(plan[0])
    whole = lambda a: pl.BlockSpec(a.shape, lambda k: (0, 0))
    any_ = pl.BlockSpec(memory_space=pl.ANY)
    D, V = pltpu.SemaphoreType.DMA, pltpu.VMEM
    token = lambda: pl.BlockSpec((rows, inner), lambda k: (0, 0))
    shape = jax.ShapeDtypeStruct
    ones = [D((hi, 1, 2))] * 4 + [D((2 * hi - 1, 1))] * 2
    many = [D((hi, chunks, 2))] * 4 + [D((2 * hi - 1, chunks))] * 2
    return pl.pallas_call(
        functools.partial(front_kernel, n, m, plan, inner, blocks),
        grid=(blocks + 2,),
        in_specs=[whole(a) for a in (gain, chan, state_p, head, hrow, gate, chans, w_dt, w_bc)] + [any_] * 4,
        out_specs=(any_,) * 6
        + (
            pl.BlockSpec((1, 128, inner), lambda k: (jnp.clip(k - 1, 0, blocks - 1), 0, 0)),
            token(), token(), token(),
            pl.BlockSpec((8, inner), lambda k: (0, 0)),
        ),
        out_shape=(
            shape((rows, inner + 384), F32), shape((rows, model), BF),
            shape((full, inner), BF), shape((full, 128), BF), shape((full, inner), BF), shape((full, inner), BF),
            shape((blocks, 128, inner), BF),
            shape((rows, inner), BF), shape((rows, inner), BF), shape((rows, inner), BF),
            shape((8, inner), F32),
        ),
        scratch_shapes=[
            V((Q + 8, inner), F32), V((Q + 8, 256), F32), V((128, inner), F32),
            V((rows, inner), F32), V((rows, inner), F32), V((rows, inner + 384), F32),
            V((full, inner), BF), V((full, 128), BF), V((full, inner), BF), V((full, inner), BF),
            V((rows, inner), F32), V((rows, inner), F32), V((rows, model), BF), V((rows, model), BF),
            V(w_zx.shape, F32), V(w_out.shape, F32),
            V((rows, 128), F32), V((rows, 128), F32), V((rows, 128), F32), V((rows, 128), F32),
            V((8, rows), F32), V((m, 8, rows), F32),
            D((10,)), D((4,)), D((m, 2)), D((m, 2)),
        ]
        + ones + many * 3,
        compiler_params=pltpu.CompilerParams(
            collective_id=cid, has_side_effects=True, vmem_limit_bytes=63 * 2**20
        ),
        name="front",
    )(gain, chan, state_p, head, hrow, gate, chans, w_dt, w_bc, tokens, cot, w_zx, w_out)


def rs_scratch(n, plan, rows, w):
    cuts, wide = plan
    chunks = len(cuts)
    hi = n // 2
    D, V = pltpu.SemaphoreType.DMA, pltpu.VMEM
    wd = max(wide, 1)
    tall = cuts[wide - 1][0] + cuts[wide - 1][1] if wide else 16
    ww = w if wide else 128
    return [
        V((hi, rows, w), BF),
        V((hi - 1, rows, w), BF),
        V((hi - 1, rows, w), BF),
        V((hi - 1, 2, tall, ww), BF),
        V((hi - 1, 2, tall, ww), BF),
        V((3, tall, ww), BF),
        D((hi, chunks)), D((hi, chunks)),
        D((hi - 1, chunks)), D((hi - 1, chunks)), D((hi - 1, chunks)), D((hi - 1, chunks)),
        D((hi - 1, 2, wd)), D((hi - 1, 2, wd)), D((hi - 1, 2, wd)), D((hi - 1, 2, wd)),
        D((2, wd)),
    ]


RS_REFS = 17


def rs_flow(n, plan, g, out, scr, shard_us, make, first_us=8, wide_us=0):
    (RX, ZR, ZL, WR, WL, WX, xs, xr, rs, rr, ls, lr, ws, wr, vs, vr, wx) = scr
    hi, z, x, mp = dp_places(n)
    rows = out.shape[0]
    cuts, wide = plan
    chunks = len(cuts)
    xp, right, left = (z * 2 + 1 - x, mp), ((z + 1) * 2 + x, mp), ((z - 1) * 2 + x, mp)
    hr, hl = z < hi - 1, z > 0
    narrow, wides = range(wide, chunks), range(wide)

    def G(zz, xx, c):
        return g.at[pl.ds(pl.multiple_of((zz * 2 + xx) * rows + cuts[c][0], 16), cuts[c][1])]

    def ch(c):
        return pl.ds(*cuts[c])

    def xcopy(tz, c):
        return put(G(tz, 1 - x, c), RX.at[tz, ch(c)], xs.at[tz, c], xr.at[tz, c], xp)

    def rcopy(tz, t, c):
        return put(RX.at[tz, ch(c)], ZR.at[t - 1, ch(c)], rs.at[t - 1, c], rr.at[t - 1, c], right)

    def lcopy(tz, t, c):
        return put(RX.at[tz, ch(c)], ZL.at[t - 1, ch(c)], ls.at[t - 1, c], lr.at[t - 1, c], left)

    def wcopy(t, lane, c, first):
        s = G(z + t, x if lane == 0 else 1 - x, c) if first else WR.at[t, lane, ch(c)]
        return put(s, WR.at[t - 1, lane, ch(c)], ws.at[t - 1, lane, c], wr.at[t - 1, lane, c], right)

    def vcopy(t, lane, c, first):
        s = G(z - t, x if lane == 0 else 1 - x, c) if first else WL.at[t, lane, ch(c)]
        return put(s, WL.at[t - 1, lane, ch(c)], vs.at[t - 1, lane, c], vr.at[t - 1, lane, c], left)

    def rrecv(t, c):
        d = ZR.at[t, ch(c)]
        return put(d, d, rs.at[t, c], rr.at[t, c], xp)

    def lrecv(t, c):
        d = ZL.at[t, ch(c)]
        return put(d, d, ls.at[t, c], lr.at[t, c], xp)

    def wrecv(t, lane, c):
        d = WR.at[t, lane, ch(c)]
        return put(d, d, ws.at[t, lane, c], wr.at[t, lane, c], xp)

    def vrecv(t, lane, c):
        d = WL.at[t, lane, ch(c)]
        return put(d, d, vs.at[t, lane, c], vr.at[t, lane, c], xp)

    def wxcopy(c):
        return put(WX.at[1, ch(c)], WX.at[2, ch(c)], wx.at[0, c], wx.at[1, c], xp)

    def start(t):
        if t == 0:
            make(z)
            for c in narrow:
                xcopy(z, c).start()
            return

        @pl.when(z + t <= hi - 1)
        def _():
            make(z + t)
            for c in narrow:
                xcopy(z + t, c).start()

        @pl.when(z - t >= 0)
        def _():
            make(z - t)
            for c in narrow:
                xcopy(z - t, c).start()

        for c in wides:
            for lane in (0, 1):
                @pl.when(z == 0)
                def _():
                    wcopy(t, lane, c, True).start()

                @pl.when(z == hi - 1)
                def _():
                    vcopy(t, lane, c, True).start()

    starts = [functools.partial(start, t) for t in range(hi - 1, -1, -1)]
    ev = []


    def wstep(t, c):
        for lane in (0, 1):
            xx = x if lane == 0 else 1 - x

            @pl.when((z + t <= hi - 1) & hl)
            def _():
                wrecv(t, lane, c).wait_recv()
                add_rows(WR.at[t, lane, ch(c)], [G(z + t, xx, c), WR.at[t, lane, ch(c)]], cuts[c][1], BF)
                wcopy(t, lane, c, False).start()

            @pl.when((z - t >= 0) & hr)
            def _():
                vrecv(t, lane, c).wait_recv()
                add_rows(WL.at[t, lane, ch(c)], [G(z - t, xx, c), WL.at[t, lane, ch(c)]], cuts[c][1], BF)
                vcopy(t, lane, c, False).start()

    def wown(c):
        for lane in (1, 0):
            xx = x if lane == 0 else 1 - x
            dst = WX.at[lane, ch(c)]

            @pl.when(hl)
            def _():
                wrecv(0, lane, c).wait_recv()

            @pl.when(hr)
            def _():
                vrecv(0, lane, c).wait_recv()

            @pl.when(hl & hr)
            def _():
                add_rows(dst, [G(z, xx, c), WR.at[0, lane, ch(c)], WL.at[0, lane, ch(c)]], cuts[c][1], BF)

            @pl.when(jnp.logical_not(hr))
            def _():
                add_rows(dst, [G(z, xx, c), WR.at[0, lane, ch(c)]], cuts[c][1], BF)

            @pl.when(jnp.logical_not(hl))
            def _():
                add_rows(dst, [G(z, xx, c), WL.at[0, lane, ch(c)]], cuts[c][1], BF)

            if lane == 1:
                wxcopy(c).start()

    def wlast(c):
        wxcopy(c).wait_recv()
        add_rows(out.at[ch(c)], [WX.at[0, ch(c)], WX.at[2, ch(c)]], cuts[c][1], F32)

    def step(t, c, to_right):
        tz = z + t if to_right else z - t
        inside = (tz <= hi - 1) if to_right else (tz >= 0)
        behind = hl if to_right else hr
        copy, recv, buf = (rcopy, rrecv, ZR) if to_right else (lcopy, lrecv, ZL)

        @pl.when(inside)
        def _():
            dst = RX.at[tz, ch(c)]
            xcopy(tz, c).wait_recv()
            if t < hi - 1:
                @pl.when(behind)
                def _():
                    recv(t, c).wait_recv()
                    add_rows(dst, [G(tz, x, c), dst, buf.at[t, ch(c)]], cuts[c][1], BF)

                @pl.when(jnp.logical_not(behind))
                def _():
                    add_rows(dst, [G(tz, x, c), dst], cuts[c][1], BF)
            else:
                add_rows(dst, [G(tz, x, c), dst], cuts[c][1], BF)
            copy(tz, t, c).start()

    def own(c):
        xcopy(z, c).wait_recv()
        base = [G(z, x, c), RX.at[z, ch(c)]]
        o = out.at[ch(c)]

        @pl.when(hl)
        def _():
            rrecv(0, c).wait_recv()

        @pl.when(hr)
        def _():
            lrecv(0, c).wait_recv()

        @pl.when(hl & hr)
        def _():
            add_rows(o, base + [ZR.at[0, ch(c)], ZL.at[0, ch(c)]], cuts[c][1], F32)

        @pl.when(jnp.logical_not(hr))
        def _():
            add_rows(o, base + [ZR.at[0, ch(c)]], cuts[c][1], F32)

        @pl.when(jnp.logical_not(hl))
        def _():
            add_rows(o, base + [ZL.at[0, ch(c)]], cuts[c][1], F32)

    unit = shard_us / rows
    narrow_rows = sum(cuts[c][1] for c in narrow)
    before = cuts[wide][0]
    slot_us = unit * narrow_rows

    def arrives(slot, c):
        return first_us + slot_us * slot + unit * (cuts[c][0] - before + cuts[c][1])

    for t in range(hi - 1, 0, -1):
        slot = min(hi - 1 - t, 2)
        if t < hi - 1:
            for c in wides:
                ev.append((first_us + slot_us * slot, functools.partial(wstep, t, c)))
        for to_right in (True, False):
            for c in narrow:
                late = 1 if t == 1 and not to_right else 0
                ev.append((arrives(slot + late, c), functools.partial(step, t, c, to_right)))
    for c in wides:
        ev.append((first_us + slot_us * (hi - 1), functools.partial(wown, c)))
    for c in narrow:
        ev.append((arrives(hi - 1, c), functools.partial(own, c)))
    for c in wides:
        ev.append((max(wide_us, arrives(hi - 1, chunks - 1) + 0.1), functools.partial(wlast, c)))

    def drain():
        for t in range(hi - 1, 0, -1):
            for c in narrow:
                @pl.when(z + t <= hi - 1)
                def _():
                    xcopy(z + t, c).wait_send()
                    rcopy(z + t, t, c).wait_send()

                @pl.when(z - t >= 0)
                def _():
                    xcopy(z - t, c).wait_send()
                    lcopy(z - t, t, c).wait_send()
            for c in wides:
                for lane in (0, 1):
                    @pl.when(z + t <= hi - 1)
                    def _():
                        wcopy(t, lane, c, True).wait_send()

                    @pl.when(z - t >= 0)
                    def _():
                        vcopy(t, lane, c, True).wait_send()
        for c in narrow:
            xcopy(z, c).wait_send()

    def drain_wide():
        for c in wides:
            wxcopy(c).wait_send()

    begins = [first_us + slot_us * max(j - 1.5, -1) for j in range(hi)]
    return ev, (drain, drain_wide), [(t, f, 1.8) for t, f in zip(begins, starts)]


def ar_scratch(chunks, rows, w):
    D, V = pltpu.SemaphoreType.DMA, pltpu.VMEM
    return [V((rows // 2, w), BF), V((rows // 2, w), BF)] + [D((chunks,))] * 7


AR_REFS = 9


def ar_flow(chunks, p, out, scr, begin, second_us, make, finish):
    (A, B, s0, r0, s1, r1, s2, r2, s3) = scr
    dp, mp = lax.axis_index("dp"), lax.axis_index("mp")
    near = (dp, mp + 1 - 2 * lax.rem(mp, 2))
    far = (dp, lax.rem(mp + 2, 4))
    half = lax.rem(mp, 2)
    rows = p.shape[0] // 2
    cr = rows // chunks

    def ch(c):
        return pl.ds(c * cr, cr)

    def row(h, c):
        return pl.multiple_of(h * rows + c * cr, cr)

    def at(ref, h, c):
        return ref.at[pl.ds(row(h, c), cr)]

    def c0(c):
        return put(at(p, 1 - half, c), A.at[ch(c)], s0.at[c], r0.at[c], near)

    def c1(c):
        return put(A.at[ch(c)], B.at[ch(c)], s1.at[c], r1.at[c], far)

    def c2(c):
        return put(B.at[ch(c)], at(out, half, c), s2.at[c], r2.at[c], near)

    def keep(c):
        return pltpu.make_async_copy(B.at[ch(c)], at(out, half, c), s3.at[c])

    def start():
        for i in range(chunks):
            c0(i).start()

    def phase(u):
        make(u * rows, rows)

        @pl.when(half != u)
        def _():
            start()

    def first(c):
        c0(c).wait_recv()
        add_rows(A.at[ch(c)], [at(p, half, c), A.at[ch(c)]], cr, BF)
        c1(c).start()

    def second(c):
        c1(c).wait_recv()
        finish(row(half, c), cr, A.at[ch(c)], B.at[ch(c)])
        c2(c).start()
        keep(c).start()

    def only(u, f, c):
        @pl.when(half == u)
        def _():
            f(c)

    ev = []
    for c in range(chunks):
        if make is None:
            ev.append((begin + 0.1 * c, functools.partial(first, c)))
            ev.append((second_us + 46 * (c + 1) / chunks, functools.partial(second, c)))
        else:
            for u in range(2):
                ev.append((begin[u] + 0.1 * c, functools.partial(only, u, first, c)))
                ev.append((second_us[u] + 23 * (c + 1) / chunks, functools.partial(only, u, second, c)))

    def sent():
        for c in range(chunks):
            c0(c).wait_send()

    def drain():
        for c in range(chunks):
            c1(c).wait_send()
            c2(c).wait_send()
            keep(c).wait()

    def arrived():
        for c in range(chunks):
            put(at(out, 1 - half, c), at(out, 1 - half, c), s2.at[c], r2.at[c], near).wait_recv()

    return ev, (start if make is None else phase), sent, drain, arrived


def product_rows(dst, d_at, d_col, lhs, rhs, rows):
    tall = min(256, rows)

    def tile(i, _):
        k = pl.multiple_of(d_at + i * tall, tall)
        a = lhs[:, pl.ds(k, tall)]
        for j, step in column_steps(rhs.shape[1]):
            v = dotf(a, rhs[:, j : j + step], ((0,), (0,)))
            dst[pl.ds(k, tall), d_col + j : d_col + j + step] = v.astype(BF)
        return 0

    lax.fori_loop(0, rows // tall, tile, 0)


def product_cols(dst, d_col, lhs, rhs, extra=None):
    def tile(j, _):
        d = pl.ds(pl.multiple_of(j * 256, 256), 256)
        dst[:, d] = dotf(lhs[...], rhs[d, :], ((1,), (1,))).astype(BF)
        return 0

    lax.fori_loop(0, rhs.shape[0] // 256, tile, 0)


T = {
    "out": 14.77,
    "out_wide": 90,
    "z": 54.99,
    "z_wide": 134.39,
    "x": 82.2,
    "s": 102.94,
    "s_pace": 8.48,
    "first1": 16.56,
    "second1": 27.21,
    "tokens": 17.24,
    "clock": 23.59,
    "x_ready": 80.16,
    "sx": [82.2, 82.3, 86, 86.1],
    "far": 82.4,
    "near": 83.49,
    "upper": 82,
    "lower": 91.42,
    "far1": 70.69,
    "near1": 81.9,
    "pz": 5,
    "step": 4.19,
    "z_own": 10.66,
    "x_own": 10.73,
    "s_sends": 85.04,
    "second_up": 92.95,
    "second_low": 105.46,
}


def back_kernel(
    n, m, plan, archunks, inner, blocks,
    xdb, before, dy, states, chan, state_p, head, hrow, gain,
    quant, cot, nout, d_z, full_out, full_z, full_x, full_s, tokens,
    g_out, g_z, g_x, g_s, block_out, input_grad, g_chan, g_state, g_head, g_row, g_gain,
    xbuf, bcbuf, dubuf, dubc, ds_ref, q_ref, r_ref,
    dxdb, dbv, dtv, dsv, fb, sb, nb, qv, cv, nv, dzv, wv, ws, go, gz, gs, p,
    lsem, bsem, free_dp, free_mp, *scr,
):
    k = pl.program_id(0)
    mp = lax.axis_index("mp")
    dp = lax.axis_index("dp")
    owned = g_out.shape[0]
    rows = tokens.shape[0]
    fine = (2 * owned) % 256 == 0
    half_rows = rows // 2
    half_at = pl.multiple_of(lax.rem(mp, 2) * half_rows, half_rows)
    hi, z, x, _ = dp_places(n)
    near = (dp, mp + 1 - 2 * lax.rem(mp, 2))
    far = (dp, lax.rem(mp + 2, 4))
    pair = mp // 2
    even = lax.rem(mp, 2) == 0
    ours = pl.ds(pl.multiple_of(pair * 128, 128), 128)
    theirs = pl.ds(pl.multiple_of((1 - pair) * 128, 128), 128)
    part = [pl.ds(u * half_rows, half_rows) for u in range(2)]

    def to_far(u):
        return put(dbv.at[part[u], theirs], fb.at[part[u]], bsem.at[0, u], bsem.at[1, u], far)

    def to_near(u):
        return put(sb.at[part[u]], nb.at[part[u]], bsem.at[2, u], bsem.at[3, u], near)

    dxv = nv

    def maker(g, lhs, rhs):
        def make(zz):
            if fine:
                product_rows(g, pl.multiple_of(zz * 2 * owned, 2 * owned), 0, lhs, rhs, 2 * owned)

        return make

    def finish_out(r, count, a, b):
        def tile(i, _):
            s = pl.ds(pl.multiple_of(i * 16, 16), 16)
            xv = cv[pl.ds(pl.multiple_of(r - half_at + i * 16, 16), 16), :]
            total = a[s, :].astype(F32) + b[s, :].astype(F32)
            b[s, :] = (xv.astype(F32) + total).astype(BF)
            return 0

        lax.fori_loop(0, count // 16, tile, 0)

    def finish_in(r, count, a, b):
        def tile(i, _):
            s = pl.ds(pl.multiple_of(i * 16, 16), 16)
            t = pl.multiple_of(r - half_at + i * 16, 16)
            xv = cv[pl.ds(t, 16), :].astype(F32)
            scale = lax.rsqrt(jnp.mean(xv * xv, axis=-1, keepdims=True) + EPS)
            xhat = xv * scale
            total = a[s, :].astype(F32) + b[s, :].astype(F32)
            e = gain[0:1, :] * total
            mean = jnp.mean(e * xhat, axis=-1, keepdims=True)
            b[s, :] = (cv[pl.ds(half_rows + t, 16), :].astype(F32) + scale * (e - xhat * mean)).astype(BF)
            v = xhat * total
            g_gain[...] += v[0:8, :] + v[8:16, :]
            return 0

        lax.fori_loop(0, count // 16, tile, 0)

    def make_in(r, count):
        a, b = dxv[pl.ds(r, count), :], dsv[pl.ds(r, count), :]

        def tile(j, _):
            d = pl.ds(pl.multiple_of(j * 256, 256), 256)
            v = dotf(a, wv[d, :], ((1,), (1,))) + dotf(b, ws[d, :], ((1,), (1,)))
            p[pl.ds(r, count), d] = (p[pl.ds(r, count), d].astype(F32) + v).astype(BF)
            return 0

        lax.fori_loop(0, wv.shape[0] // 256, tile, 0)

    def sum_far(u):
        to_far(u).wait_recv()
        r = part[u]
        sb[r, :] = (dbv[r, ours].astype(F32) + fb[r, :].astype(F32)).astype(BF)
        to_near(u).start()

    def sum_near(u):
        to_near(u).wait_recv()

        def tile(i, _):
            r = pl.ds(pl.multiple_of(i * 128, 128), 128)
            v = sb[r, :].astype(F32) + nb[r, :].astype(F32)
            v = jnp.where(even, pltpu.roll(v, 64, 1), v)
            dsv[r, :] = jnp.where(lanes_below(128, 64), dtv[r, :].astype(F32), v).astype(BF)
            return 0

        tiles = half_rows // 128
        lax.fori_loop(u * tiles, (u + 1) * tiles, tile, 0)

    set_a, rest = scr[:RS_REFS], scr[RS_REFS:]
    set_b, rest = rest[:RS_REFS], rest[RS_REFS:]
    set_s, rest = rest[:RS_REFS], rest[RS_REFS:]
    wides_x, rest = rest[:3], rest[3:]
    sems_x, rest = rest[: RS_REFS - 6], rest[RS_REFS - 6 :]
    ar_a, sems_in = rest[:AR_REFS], rest[AR_REFS:]
    set_x = tuple(set_a[:3]) + tuple(wides_x) + tuple(sems_x)
    ar_b = tuple(ar_a[:2]) + tuple(sems_in)
    eo, drain_o, so = rs_flow(n, plan, go, g_out, set_a, 11.3, maker(go, cv, nv), T["out"], T["out_wide"])
    ez, drain_z, sz = rs_flow(n, plan, gz, g_z, set_b, 11.3, maker(gz, qv, dzv), T["z"], T["z_wide"])
    ex, drain_x, sx = rs_flow(n, plan, go, g_x, set_x, 11.3, maker(go, qv, dxv), T["x"])
    es, drain_s, ss = rs_flow(n, cuts_of(owned, True), gs, g_s, set_s, T["s_pace"], lambda zz: None, T["s"])
    e1, start1, sent1, drain1, arrived1 = ar_flow(archunks, p, block_out, ar_a, T["first1"], T["second1"], None, finish_out)
    e2, start2, sent2, drain2, arrived2 = ar_flow(
        archunks, p, input_grad, ar_b, (T["lower"] + 0.1, T["upper"] + 0.1), (T["second_low"], T["second_up"]), make_in, finish_in
    )

    def load(src, dst, i):
        return pltpu.make_async_copy(src, dst, lsem.at[i])

    load_c, load_n = load(cot, cv, 0), load(nout, nv, 1)
    load_wo, load_q, load_dz = load(full_out, wv, 2), load(quant, qv, 3), load(d_z, dzv, 4)
    load_wz, load_wx, load_ws = load(full_z, wv, 5), load(full_x, wv, 6), load(full_s, ws, 7)
    mine = pl.ds(half_at, half_rows)
    load_t = load(tokens.at[mine], cv.at[pl.ds(0, half_rows)], 8)
    load_g = load(cot.at[mine], cv.at[pl.ds(half_rows, half_rows)], 9)

    def whole_product(g, lhs, rhs):
        if not fine:
            product_rows(g, 0, 0, lhs, rhs, g.shape[0])

    def prologue():
        bar = pltpu.get_barrier_semaphore()
        count = signal_dp(n, bar)
        for d in (near, far):
            pl.semaphore_signal(bar, inc=1, device_id=d, device_id_type=MESH)
        for copy in (load_c, load_n, load_wo, load_q, load_dz, load_ws):
            copy.start()
        g_gain[...] = jnp.zeros_like(g_gain)
        pl.semaphore_wait(bar, count + 2)
        load_c.wait()
        load_n.wait()
        whole_product(go, cv, nv)
        so[0][1]()
        load_wo.wait()
        product_cols(p, 0, nv, wv)
        load_wz.start()
        start1()
        for e in so[1:]:
            e[1]()
        tokens_load()
        z_ready()
        for e in sz:
            e[1]()

    def tokens_load():
        load_t.start()
        load_g.start()

    def z_ready():
        load_q.wait()
        load_dz.wait()
        whole_product(gz, qv, dzv)

    def z_branch():
        sent1()
        load_wz.wait()
        product_cols(p, 0, dzv, wv)
        load_wx.start()

    def tokens_in():
        load_t.wait()
        load_g.wait()

    def next_sums():
        drain1()
        for d in (near, far):
            pl.semaphore_signal(free_mp, inc=1, device_id=d, device_id_type=MESH)

    def next_rows():
        drain_o[0]()
        pl.semaphore_signal(free_dp, inc=1, device_id=(z * 2 + 1 - x, mp), device_id_type=MESH)

        @pl.when(z > 0)
        def _():
            pl.semaphore_signal(free_dp, inc=1, device_id=((z - 1) * 2 + x, mp), device_id_type=MESH)

        @pl.when(z < hi - 1)
        def _():
            pl.semaphore_signal(free_dp, inc=1, device_id=((z + 1) * 2 + x, mp), device_id_type=MESH)

    def input_part(u):
        if u == 1:
            load_wx.wait()
            pl.semaphore_wait(free_mp, 2)
        start2(u)

    def s_sends():
        product_rows(gs, 0, 0, qv, dsv, gs.shape[0])
        for e in ss:
            e[1]()

    def x_ready():
        pl.semaphore_wait(free_dp, 1 + (z > 0).astype(jnp.int32) + (z < hi - 1).astype(jnp.int32))
        whole_product(go, qv, dxv)

    def ordered(*lists):
        return sorted([e for q in lists for e in q], key=lambda e: e[0])

    o_last = max(t for t, f in eo if f.func.__name__ == "own")
    one_last = max(t for t, _ in e1)
    def shift(events, by):
        return [(t + (by if f.func.__name__ in ("own", "wown", "wlast") else 0), f) for t, f in events]

    ez, ex = shift(ez, T["z_own"]), shift(ex, T["x_own"])
    early = ordered(eo, ez, e1, [(T["tokens"], tokens_in), (o_last + 0.1, next_rows), (one_last + 0.1, next_sums)])
    late = [
        (T["x_ready"], x_ready), (T["far"], functools.partial(sum_far, 0)), (T["near"], functools.partial(sum_near, 0)),
        (T["upper"], functools.partial(input_part, 1)), (T["lower"], functools.partial(input_part, 0)),
        (T["s_sends"], s_sends),
    ]
    sx = [(t, *e[1:]) for t, e in zip(T["sx"] + T["sx"][-1:] * len(sx), sx)]
    fixed = {blocks // 2: [functools.partial(lambda u: to_far(u).start(), 1)]}
    fixed.setdefault(T["pz"], []).append(z_branch)
    late += [(T["far1"], functools.partial(sum_far, 1)), (T["near1"], functools.partial(sum_near, 1))]
    pl.when(k == 0)(prologue)
    at = 0
    clock = T["clock"]
    for i in range(blocks):
        end = at
        while end < len(early) and early[end][0] <= clock:
            clock += early[end][2] if len(early[end]) > 2 else 0.2
            end += 1
        for f in fixed.get(i, []):
            pl.when(k == i)(f)
        clock += T["step"] + (6.6 if i == T["pz"] else 0)
        if end > at:
            @pl.when(k == i)
            def _():
                for e in early[at:end]:
                    e[1]()
        at = end

    scan_bwd_kernel(
        inner, blocks, xdb, before, dy, states, chan, state_p, head, hrow,
        dxdb, g_chan, g_state, g_head, g_row,
        xbuf, bcbuf, dubuf, dubc, ds_ref, q_ref, r_ref,
    )
    here = pl.ds(pl.multiple_of((blocks - 1 - k) * Q, Q), Q)
    dxv[here, :] = dxdb[:, 0:inner]
    dtv[here, :] = dxdb[:, inner : inner + 128]
    dbv[here, :] = dxdb[:, inner + 128 :]

    @pl.when(k == blocks - 1)
    def _():
        to_far(0).start()
        load_ws.wait()
        for e in ordered(early[at:], late, ex, sx, es, e2):
            e[1]()
        drain_o[1]()
        for flow in (drain_z, drain_x, drain_s):
            flow[0]()
            flow[1]()
        sent2()
        drain2()
        arrived1()
        arrived2()
        for u in range(2):
            to_far(u).wait_send()
            to_near(u).wait_send()


def back(xdb, dy, states, chan, state_p, head, hrow, gain, quant, cot, nout, d_z, full_out, full_z, full_x, full_s, tokens, n, m, archunks, cid):
    rows, width = xdb.shape
    inner = chan.shape[1]
    model = tokens.shape[1]
    blocks = rows // Q
    full = full_out.shape[0]
    owned = full // n
    plan = cuts_of(owned)
    whole = lambda a: pl.BlockSpec(a.shape, lambda s: (0, 0))
    rev = lambda s: (blocks - 1 - s, 0)
    acc = lambda r, w: pl.BlockSpec((r, w), lambda s: (0, 0))
    any_ = pl.BlockSpec(memory_space=pl.ANY)
    V, D = pltpu.VMEM, pltpu.SemaphoreType.DMA
    set_a = rs_scratch(n, plan, owned, inner)
    ar_a = ar_scratch(archunks, rows, model)
    sums = [(owned, inner)] * 3 + [(owned, 128)]
    smalls = [(8 * CONV + 8, inner), (8 * CONV + 8, 256), (24, 128), (16, inner), (8, model)]
    return pl.pallas_call(
        functools.partial(back_kernel, n, m, plan, archunks, inner, blocks),
        grid=(blocks,),
        in_specs=[
            pl.BlockSpec((Q, width), rev),
            pl.BlockSpec((8, width), lambda s: (jnp.maximum((blocks - 1 - s) * (Q // 8) - 1, 0), 0)),
            pl.BlockSpec((Q, inner), rev),
            pl.BlockSpec((1, 128, inner), lambda s: (blocks - 1 - s, 0, 0)),
            whole(chan), whole(state_p), whole(head), whole(hrow), whole(gain),
        ]
        + [any_] * 9,
        out_specs=tuple(acc(*s) for s in sums) + (any_, any_) + tuple(acc(*s) for s in smalls),
        out_shape=tuple(jax.ShapeDtypeStruct(s, F32) for s in sums)
        + (jax.ShapeDtypeStruct(tokens.shape, BF),) * 2
        + tuple(jax.ShapeDtypeStruct(s, F32) for s in smalls),
        scratch_shapes=[
            V((Q + 8, inner), F32), V((Q + 8, 256), F32), V((Q + 8, inner), F32), V((Q + 8, 256), F32),
            V((128, inner), F32), V((Q, inner), F32), V((Q, inner), BF),
            V((Q, width), BF), V((rows, 256), BF), V((rows, 128), BF), V((rows, 128), BF),
            V((rows, 128), BF), V((rows, 128), BF), V((rows, 128), BF),
            V(quant.shape, BF), V(cot.shape, BF), V(nout.shape, BF), V(d_z.shape, BF),
            V(full_out.shape, BF), V(full_s.shape, BF),
            V((full, inner), BF), V((full, inner), BF), V((full, 128), BF), V(tokens.shape, BF),
            D((10,)), D((4, 2)), pltpu.SemaphoreType.REGULAR, pltpu.SemaphoreType.REGULAR,
        ]
        + set_a
        + rs_scratch(n, plan, owned, inner)
        + rs_scratch(n, cuts_of(owned, True), owned, 128)
        + set_a[3:]
        + ar_a
        + ar_a[2:],
        compiler_params=pltpu.CompilerParams(
            collective_id=cid, has_side_effects=True, vmem_limit_bytes=63 * 2**20
        ),
        name="back",
    )(xdb, xdb, dy, states, chan, state_p, head, hrow, gain, quant, cot, nout, d_z, full_out, full_z, full_x, full_s, tokens)


def adam_step(weight, grad, first, second, rate, shrink):
    first = BETA_FIRST * first + (1.0 - BETA_FIRST) * grad
    second = BETA_SECOND * second + (1.0 - BETA_SECOND) * grad * grad
    fix_first = 1.0 - BETA_FIRST**STEP
    fix_second = 1.0 - BETA_SECOND**STEP
    update = first / fix_first / (jnp.sqrt(second / fix_second) + ADAM_EPS) + shrink * weight
    return (weight - rate * update, first, second)


def column_steps(width, step=512):
    return [(j, min(step, width - j)) for j in range(0, width, step)]


def lanes_below(rows, count):
    return lax.broadcasted_iota(jnp.int32, (rows, 128), 1) < count


def square_rows(ref, width):
    def body(i, acc):
        v = ref[pl.ds(pl.multiple_of(i * 8, 8), 8), 0:width]
        v = v * v
        for k in range(width // 128):
            acc = acc + v[:, k * 128 : (k + 1) * 128]
        return acc

    return lax.fori_loop(0, ref.shape[0] // 8, body, jnp.zeros((8, 128), F32))


def tail_kernel(
    n, m, inner, model,
    gz, go, gx, gs, g_chan, g_gate, g_gain, g_state, g_head,
    vec_out, bc_out, norm_out,
    dbuf, mbuf, bcbuf, vs, vr, bs, br, ts, tr,
):
    dp = lax.axis_index("dp")
    mp = lax.axis_index("mp")
    bar = pltpu.get_barrier_semaphore()
    dps = [lax.rem(dp + k, n) for k in range(1, n)]
    mps = [lax.rem(mp + k, m) for k in range(1, m)]
    for d in dps:
        pl.semaphore_signal(bar, inc=1, device_id=(d, mp), device_id_type=MESH)
    for d in mps:
        pl.semaphore_signal(bar, inc=1, device_id=(dp, d), device_id_type=MESH)
    mine = dbuf.at[dp]
    at_gain = 6 * inner // 128
    at_state = at_gain + model // 128
    at_head = at_state + 10
    at_sq = dbuf.shape[1] - 8

    def rows_of(value, row):
        for j in range(value.shape[1] // 128):
            mine[row + j : row + j + 1, :] = value[:, j * 128 : (j + 1) * 128]

    def folded(ref, i):
        return jnp.sum(ref[8 * i : 8 * i + 8, :], axis=0, keepdims=True)

    for q in range(CONV + 1):
        rows_of(folded(g_chan, q), q * inner // 128)
        rows_of(folded(g_state, q), at_state + 2 * q)
    rows_of(folded(g_gate, 0), (CONV + 1) * inner // 128)
    rows_of(folded(g_gain, 0) * (mp < 2).astype(F32), at_gain)
    for q in range(3):
        mine[at_head + q : at_head + q + 1, :] = folded(g_head, q)
    mine[at_head + 3 : at_sq, :] = jnp.zeros((at_sq - at_head - 3, 128), F32)
    mine[at_sq:, :] = square_rows(gz, inner) + square_rows(go, inner) + square_rows(gx, inner) + square_rows(gs, 128)
    bcbuf[mp] = gs[...]
    pl.semaphore_wait(bar, n + m - 2)

    def to_dp(d):
        return put(dbuf.at[dp], dbuf.at[dp], vs.at[d], vr.at[dp], (d, mp))

    def from_dp(d):
        return put(dbuf.at[d], dbuf.at[d], vs.at[d], vr.at[d], (d, mp))

    def to_mp(buf, d, s, r):
        return put(buf.at[mp], buf.at[mp], s.at[d], r.at[mp], (dp, d))

    def from_mp(buf, d, s, r):
        return put(buf.at[d], buf.at[d], s.at[d], r.at[d], (dp, d))

    for d in dps:
        to_dp(d).start()
    for d in mps:
        to_mp(bcbuf, d, bs, br).start()
    for d in dps:
        from_dp(d).wait_recv()
    total = dbuf[0]
    for d in range(1, n):
        total = total + dbuf[d]
    mbuf[mp] = total
    for d in mps:
        to_mp(mbuf, d, ts, tr).start()
    for d in mps:
        from_mp(bcbuf, d, bs, br).wait_recv()
    below = lanes_below(bc_out.shape[0], 64)
    for q in range(m // 2):
        bc_out[:, q * 128 : (q + 1) * 128] = jnp.where(below, pltpu.roll(bcbuf[2 * q], 64, 1), bcbuf[2 * q + 1])
    for d in mps:
        from_mp(mbuf, d, ts, tr).wait_recv()

    def over_mp(a, b):
        v = mbuf[0, a:b, :]
        for d in range(1, m):
            v = v + mbuf[d, a:b, :]
        return v

    per = inner // 128
    start = model // 128
    vec_out[0:start, :] = over_mp(at_gain, at_state)
    for q in range(6):
        for d in range(m):
            at = start + (q * m + d) * per
            vec_out[at : at + per, :] = mbuf[d, q * per : (q + 1) * per, :]
    end = start + 6 * m * per
    vec_out[end : end + 10, :] = over_mp(at_state, at_head)
    heads = inner // 64
    low = lanes_below(1, heads)
    lines = [jnp.zeros((1, 128), F32), jnp.zeros((1, 128), F32)]
    for q in range(3):
        for d in range(m):
            v = jnp.where(low, mbuf[d, at_head + q : at_head + q + 1, :], 0.0)
            spot = q * heads * m + d * heads
            lines[spot // 128] = lines[spot // 128] + (pltpu.roll(v, spot % 128, 1) if spot % 128 else v)
    vec_out[end + 10 : end + 11, :] = lines[0]
    vec_out[end + 11 : end + 12, :] = lines[1]
    vec_out[end + 12 :, :] = jnp.zeros((vec_out.shape[0] - end - 12, 128), F32)
    squares = over_mp(at_sq, at_sq + 8) + square_rows(vec_out, 128)
    squares = jnp.sum(jnp.sum(squares, axis=1, keepdims=True), axis=0, keepdims=True)
    norm_out[...] = jnp.sqrt(jnp.broadcast_to(squares, (8, 128)))
    for d in dps:
        to_dp(d).wait_send()
    for d in mps:
        to_mp(bcbuf, d, bs, br).wait_send()
        to_mp(mbuf, d, ts, tr).wait_send()


def tail_sums(gz, go, gx, gs, g_chan, g_gate, g_gain, g_state, g_head, n, m, cid):
    V = pl.BlockSpec(memory_space=pltpu.VMEM)
    D = pltpu.SemaphoreType.DMA
    owned, inner = gx.shape
    model = g_gain.shape[1]
    rows = -(-(6 * inner // 128 + model // 128 + 13) // 8) * 8 + 8
    total = -(-(model // 128 + 6 * m * inner // 128 + 12) // 8) * 8
    return pl.pallas_call(
        functools.partial(tail_kernel, n, m, inner, model),
        in_specs=[V] * 9,
        out_specs=(V, V, V),
        out_shape=(
            jax.ShapeDtypeStruct((total, 128), F32),
            jax.ShapeDtypeStruct((owned, 256), F32),
            jax.ShapeDtypeStruct((8, 128), F32),
        ),
        scratch_shapes=[
            pltpu.VMEM((n, rows, 128), F32),
            pltpu.VMEM((m, rows, 128), F32),
            pltpu.VMEM((m, owned, 128), F32),
            D((n,)), D((n,)), D((m,)), D((m,)), D((m,)), D((m,)),
        ],
        compiler_params=pltpu.CompilerParams(
            collective_id=cid, has_side_effects=True, vmem_limit_bytes=62 * 2**20
        ),
        name="tail_sums",
    )(gz, go, gx, gs, g_chan, g_gate, g_gain, g_state, g_head)


def adam_kernel(
    inner, heads, blocks,
    norm, gz, go, gx, gs, gbc, block_in, grad_in,
    wz, mz, vz, wd, md, vd, wb, mb, vb, wo, mo, vo,
    nwz, nmz, nvz, nwd, nmd, nvd, nwb, nmb, nvb, nwo, nmo, nvo, block_out, grad_out,
    flat,
):
    step = pl.program_id(0)
    clip = CLIP / jnp.maximum(norm[0:1, 0:1], CLIP)
    rows = gx.shape[0]
    lanes = inner // 128
    block_out[...] = block_in[...]
    grad_out[...] = grad_in[...]

    def update(g, w, mo_, vo_, outs, where):
        new = adam_step(w, g * clip, mo_, vo_, RATE_MATRIX, DECAY_MATRIX)
        for ref, v in zip(outs, new, strict=True):
            ref[where] = v

    for i in range(rows // 8):
        for j in range(lanes):
            cols = slice(j * 128, (j + 1) * 128)
            at = i * 16 * lanes + 2 * j
            flat[pl.ds(at, 8, stride=2 * lanes), :] = gz[8 * i : 8 * i + 8, cols]
            flat[pl.ds(at + 1, 8, stride=2 * lanes), :] = gx[8 * i : 8 * i + 8, cols]

    def zx(i, _):
        s = pl.ds(pl.multiple_of(i * 64, 64), 64)
        update(flat[s, :], wz[s, :], mz[s, :], vz[s, :], (nwz, nmz, nvz), (s, slice(None)))
        return 0

    lax.fori_loop(0, flat.shape[0] // 64, zx, 0, unroll=4)

    def outer(i, _):
        s = pl.ds(pl.multiple_of(i * 8, 8), 8)
        update(go[s, :], wo[s, :], mo[s, :], vo[s, :], (nwo, nmo, nvo), (s, slice(None)))
        return 0

    lax.fori_loop(0, rows // 8, outer, 0, unroll=4)
    update(gbc[...], wb[...], mb[...], vb[...], (nwb, nmb, nvb), (slice(None), slice(None)))

    @pl.when(step == blocks - 1)
    def _():
        g = gs[...].T[0:heads, :]
        update(g, wd[...], md[...], vd[...], (nwd, nmd, nvd), (slice(None), slice(None)))


def adam(norm, gz, go, gx, gs, gbc, block_out, input_grad, groups):
    owned, inner = gx.shape
    heads = groups[1][0].shape[0]
    step = 32
    args = [norm, gz, go, gx, gs, gbc, block_out, input_grad] + [a for group in groups for a in group]

    def spec(a):
        return pl.BlockSpec((a.shape[0] * step // owned, a.shape[1]), lambda i: (i, 0))

    def whole(a):
        return pl.BlockSpec(a.shape, lambda i: (0, 0))

    states = args[8:]
    specs = [whole(a) if i in (3, 4, 5) else spec(a) for i, a in enumerate(states)]
    moved = (block_out, input_grad)
    return pl.pallas_call(
        functools.partial(adam_kernel, inner, heads, owned // step),
        grid=(owned // step,),
        in_specs=[whole(norm), spec(gz), spec(go), spec(gx), whole(gs), spec(gbc)] + [spec(a) for a in moved] + specs,
        out_specs=tuple(specs) + tuple(spec(a) for a in moved),
        out_shape=tuple(jax.ShapeDtypeStruct(a.shape, F32) for a in states)
        + tuple(jax.ShapeDtypeStruct(a.shape, a.dtype) for a in moved),
        scratch_shapes=[pltpu.VMEM((step * 2 * inner // 128, 128), F32)],
        compiler_params=pltpu.CompilerParams(vmem_limit_bytes=62 * 2**20),
        name="adam",
    )(*args)


def pad_rows(a, rows=8):
    return jnp.concatenate([a, jnp.zeros((rows - a.shape[0], a.shape[1]), a.dtype)], axis=0)


def on_device(
    tokens,
    cotangent,
    seq_level,
    w_zx,
    w_dt,
    w_bc,
    w_out,
    vectors,
    m_zx,
    m_dt,
    m_bc,
    m_out,
    m_vec,
    v_zx,
    v_dt,
    v_bc,
    v_out,
    v_vec,
):
    mp_rank = lax.axis_index("mp")
    mp_count = lax.axis_size("mp")
    dp_count = lax.axis_size("dp")
    row_count, model_dim = tokens.shape
    owned = w_zx.shape[0]
    local_inner = w_zx.shape[2]
    inner = local_inner * mp_count
    local_heads = w_dt.shape[1]
    all_heads = local_heads * mp_count
    head_dim = inner // all_heads
    state_dim = w_bc.shape[1] // 2
    gain_in = vectors[:model_dim]
    chan_all = vectors[model_dim : model_dim + 6 * inner].reshape(6, inner)
    chan_loc = lax.dynamic_slice_in_dim(chan_all, mp_rank * local_inner, local_inner, 1)
    state_start = model_dim + 6 * inner
    state_vec = vectors[state_start : state_start + 10 * state_dim].reshape(5, 2 * state_dim)
    head_start = state_start + 10 * state_dim
    head_all = vectors[head_start : head_start + 3 * all_heads].reshape(3, all_heads)
    head_loc = lax.dynamic_slice_in_dim(head_all, mp_rank * local_heads, local_heads, 1)
    active = jnp.left_shift(jnp.int32(all_heads // 8), seq_level[0])
    head_ids = mp_rank * local_heads + jnp.arange(local_heads)
    head_mask = (head_ids < active).astype(F32)
    mask_row = jnp.repeat(head_mask, head_dim)
    chan8 = pad_rows(chan_loc[:5])
    state8 = pad_rows(state_vec)
    head8 = pad_rows(jnp.pad(head_loc[:2], ((0, 0), (0, 128 - local_heads))))
    hrow8 = pad_rows(jnp.stack([jnp.repeat(head_loc[2], head_dim), mask_row]))
    gain8 = pad_rows(gain_in[None])
    channels = (active * head_dim).astype(F32)
    gate8 = pad_rows(chan_loc[5:6])
    per = jnp.full((8, 128), 1.0, F32) / channels

    def flat(a):
        return jnp.swapaxes(a.reshape(owned, 2, local_inner // 128, 128), 1, 2).reshape(-1, 128)

    xdb, quant, full_x, full_s, full_z, full_out, states, normed_out, d_z, d_y, g_gate = front(
        tokens, cotangent, gain8, chan8, state8, head8, hrow8, gate8, per, flat(w_zx), w_out, w_dt.T, w_bc,
        dp_count, mp_count, 1,
    )
    g_out, g_z, g_x, g_s, block_out, input_grad, g_chan, g_state, g_head, g_row, g_gain = back(
        xdb, d_y, states, chan8, state8, head8, hrow8, gain8, quant, cotangent, normed_out, d_z,
        full_out, full_z, full_x, full_s, tokens, dp_count, mp_count, 4, 3,
    )
    vec, g_bc, norm = tail_sums(
        g_z, g_out, g_x, g_s, g_chan, g_gate, g_gain, g_state, g_head, dp_count, mp_count, 5
    )
    grad_norm = norm[0, 0]

    def unflat(a):
        return jnp.swapaxes(a.reshape(owned, local_inner // 128, 2, 128), 1, 2).reshape(w_zx.shape)

    groups = (
        tuple(flat(a) for a in (w_zx, m_zx, v_zx)),
        (w_dt.T, m_dt.T, v_dt.T),
        (w_bc, m_bc, v_bc),
        (w_out, m_out, v_out),
    )
    *new, block_out, input_grad = adam(norm, g_z, g_out, g_x, g_s, g_bc, block_out, input_grad, groups)
    clip = CLIP / jnp.maximum(grad_norm, CLIP)
    small = vec.reshape(-1)[: vectors.shape[0]]
    new_vec = adam_step(vectors, small * clip, m_vec, v_vec, RATE_VECTOR, 0.0)
    new_zx = (unflat(a) for a in new[:3])
    new_dt = (a.T for a in new[3:6])
    return (block_out, input_grad, grad_norm, *new_zx, *new_dt, *new[6:], *new_vec)


def solution(mesh):
    placed = (
        P("dp", None),
        P("dp", None),
        P("dp"),
        P("dp", None, "mp"),
        P("dp", "mp"),
        P("dp", None),
        P("dp", "mp"),
        P(),
        P("dp", None, "mp"),
        P("dp", "mp"),
        P("dp", None),
        P("dp", "mp"),
        P(),
        P("dp", None, "mp"),
        P("dp", "mp"),
        P("dp", None),
        P("dp", "mp"),
        P(),
    )
    return jax.shard_map(
        on_device,
        mesh=mesh,
        in_specs=placed,
        out_specs=(
            P("dp", None),
            P("dp", None),
            P(),
            P("dp", None, "mp"),
            P("dp", None, "mp"),
            P("dp", None, "mp"),
            P("dp", "mp"),
            P("dp", "mp"),
            P("dp", "mp"),
            P("dp", None),
            P("dp", None),
            P("dp", None),
            P("dp", "mp"),
            P("dp", "mp"),
            P("dp", "mp"),
            P(),
            P(),
            P(),
        ),
        check_vma=False,
    )
```
